512 devices in a mesh: pipe: 16 (over z), expert: 32 (over x, y, core).
Axes of the slice: x: 4, y: 4, z: 16, core: 2. Of those that a mesh axis runs over, the one named last changes fastest.
Arguments:
- forward_in: bfloat16 [16, 256, 3584], P('pipe', 'expert'), may hold values from -6 to 6
- forward_new: bfloat16 [1, 256, 3584], P(None, 'expert'), may hold values from -6 to 6
- grad_in: bfloat16 [16, 256, 3584], P('pipe', 'expert'), may hold values from -6 to 6
- grad_new: bfloat16 [1, 256, 3584], P(None, 'expert'), may hold values from -6 to 6
- saved_inputs: bfloat16 [2, 16, 256, 3584], P(None, 'pipe', 'expert'), may hold values from -6 to 6
- forward_ids: int32 [2, 16, 256, 2], P(None, 'pipe', 'expert'), may hold values from 0 to 3, all different within a row; in each aligned block of 8 rows (0 to 7, 8 to 15, ..., all dimensions but the last counted through in order) at most 6 rows name the same one
- backward_ids: int32 [2, 16, 256, 2], P(None, 'pipe', 'expert'), may hold values from 0 to 3, all different within a row; in each aligned block of 8 rows (0 to 7, 8 to 15, ..., all dimensions but the last counted through in order) at most 6 rows name the same one
- norm_gain: bfloat16 [16, 3584], P('pipe'), may hold values from 0.5 to 1.5
- router: bfloat16 [16, 3584, 4], P('pipe'), may hold values from -0.09375 to 0.09375
- gate_proj: bfloat16 [16, 3584, 4096], P('pipe', None, 'expert'), may hold values from -0.09375 to 0.09375
- up_proj: bfloat16 [16, 3584, 4096], P('pipe', None, 'expert'), may hold values from -0.09375 to 0.09375
- down_proj: bfloat16 [16, 4096, 3584], P('pipe', 'expert'), may hold values from -0.1875 to 0.1875
Outputs:
- forward_out: bfloat16 [2, 16, 256, 3584], P(None, 'pipe', 'expert')
- input_grads: bfloat16 [2, 16, 256, 3584], P(None, 'pipe', 'expert')
The draws below stay inside these ranges and needn't reach their ends.
Inputs may be any that keep to these rules, and one draw needn't show every extreme that they name: `forward_ids`: each token names 2 different experts. Within the 8 rows of one device (aligned blocks along all leading dimensions) no expert is named more than 6 times, and in every draw some block names some expert exactly 6 times. `backward_ids`: as for forward_ids.
All inputs are finite; a program needn't handle non-finite values.
Results may differ from the reference program's by a relative error of at most 0.02.
Values may be sent and summed in bfloat16 or wider, within the bound.
No kernel may reach another device: no remote copies, remote signals or barrier semaphores. Data moves between devices by JAX's collectives and lax.ppermute only.
A program may use at most 128 MiB of HBM per device.

```python
import math
import jax
import jax.numpy as jnp
import numpy as np
from jax import lax

D = 3584
FF = 1024
EXPERTS = 4
TOPK = 2
MICRO = 2
TOK_DEV = 8
SECTIONS = 16
TOKENS = 256
CAP = 6
N_EXPERT = 32


def steps_of(stream_key, dims, split, low, largest):
    loudness = 1.0
    for position, parts in split:
        draws = jax.random.uniform(jax.random.fold_in(jax.random.fold_in(stream_key, 6), position), (parts,), jnp.float32, low / len(split), largest / len(split))
        loudness = loudness * jnp.repeat(jnp.exp(draws), dims[position] // parts).reshape((-1,) + (1,) * (len(dims) - 1 - position))
    return loudness


def routed_block(own_key, own, number, rows, amount, top, bound, lean):
    order = jax.random.permutation(own_key, amount)
    heavy_load, usual = load_shares(amount, rows * top, bound, lean, True), load_shares(amount, rows * top, bound, lean, False)
    places = jnp.arange(amount)

    def named(sizes, rotation):
        used = int((sizes > 0).sum())
        fixed = max(1, used // 4)
        passed = fixed + (places - fixed + rotation * (used - fixed)) % max(1, amount - fixed)
        return jnp.zeros((amount,), jnp.int32).at[order[jnp.where(places < fixed, places, passed)]].set(jnp.asarray(sizes, jnp.int32))

    sizes = jnp.where(number % 4 == 0, named(heavy_load, number // 4), named(usual, number - number // 4 - 1))
    mixed = jax.random.permutation(jax.random.fold_in(own, 3), amount)
    donor, taker = mixed[0:amount // 2 * 2:2], mixed[1:amount // 2 * 2:2]
    room = jnp.minimum(sizes[donor] - 1, bound - sizes[taker]) // 2
    room = jnp.where((donor == order[0]) | (taker == order[0]) | (sizes[taker] == 0), 0, jnp.maximum(room, 0))
    passed = jax.random.randint(jax.random.fold_in(own, 4), (amount // 2,), 0, 1 << 20) % (room + 1)
    sizes = sizes.at[donor].add(-passed).at[taker].add(passed)
    members = jnp.searchsorted(jnp.cumsum(sizes), jnp.arange(rows * top), side="right").astype(jnp.int32)
    table = members.reshape(top, rows).T
    table = table[jax.random.permutation(jax.random.fold_in(own, 1), rows)]
    rotation = jax.random.randint(jax.random.fold_in(own, 2), (rows, 1), 0, top)
    return jnp.take_along_axis(table, (jnp.arange(top)[None, :] + rotation) % top, axis=1)


def load_shares(count, total, bound, skew, full):
    portions = [(1 << 20) // math.isqrt(rank ** skew) + 1 for rank in range(1, count + 1)]
    largest = bound if full else min(bound, max(-(-total // count), total * portions[0] // sum(portions)))
    least = 1 if total - largest >= count - 1 else 0
    given, spare = [largest] + [least] * (count - 1), total - largest - least * (count - 1)
    while spare > 0:
        free = [i for i in range(1, count) if given[i] < largest] or [i for i in range(1, count) if given[i] < bound]
        pool, left = sum([portions[i] for i in free]), spare
        for i in free:
            more = min(bound - given[i], max(1, left * portions[i] // pool), spare)
            given[i] = given[i] + more
            spare = spare - more
    return np.array(given)


def scatter_about(own_key, extent, scale, most, split=(), kind=jnp.bfloat16):
    values = jax.random.normal(own_key, extent, jnp.float32) * scale
    if len(split) > 0:
        values = steps_of(own_key, extent, split, -0.22, 0.18) * values
    return jnp.clip(values, min=-most, max=most).astype(kind)


def setup_inputs(seed: int = 0) -> dict:
    key_list = jax.random.split(jax.random.key(seed), 13)
    forward_in = scatter_about(key_list[0], (SECTIONS, TOKENS, D), 1.0, 6.0, ((0, 16), (1, 32)))
    forward_new = scatter_about(key_list[1], (MICRO - 1, TOKENS, D), 1.0, 6.0, ((1, 32),))
    grad_in = scatter_about(key_list[2], (SECTIONS, TOKENS, D), 1.0, 6.0, ((0, 16), (1, 32)))
    grad_new = scatter_about(key_list[3], (MICRO - 1, TOKENS, D), 1.0, 6.0, ((1, 32),))
    saved_inputs = scatter_about(key_list[4], (MICRO, SECTIONS, TOKENS, D), 1.0, 6.0, ((1, 16), (2, 32)))
    forward_ids_keys = jax.random.split(jax.random.fold_in(key_list[5], 1), MICRO * SECTIONS * TOKENS // TOK_DEV)
    forward_ids_turns = jax.random.permutation(jax.random.fold_in(key_list[5], 3), MICRO * SECTIONS * TOKENS // TOK_DEV)
    forward_ids = jax.vmap(lambda own, number: routed_block(jax.random.fold_in(key_list[5], 2), own, number, TOK_DEV, EXPERTS, TOPK, CAP, 2))(forward_ids_keys, forward_ids_turns).reshape((MICRO, SECTIONS, TOKENS, TOPK))
    backward_ids_keys = jax.random.split(jax.random.fold_in(key_list[6], 1), MICRO * SECTIONS * TOKENS // TOK_DEV)
    backward_ids_turns = jax.random.permutation(jax.random.fold_in(key_list[6], 3), MICRO * SECTIONS * TOKENS // TOK_DEV)
    backward_ids = jax.vmap(lambda own, number: routed_block(jax.random.fold_in(key_list[6], 2), own, number, TOK_DEV, EXPERTS, TOPK, CAP, 2))(backward_ids_keys, backward_ids_turns).reshape((MICRO, SECTIONS, TOKENS, TOPK))
    norm_gain = jnp.clip(1.0 + 0.1 * jax.random.normal(key_list[7], (SECTIONS, D), jnp.float32), 0.5, 1.5).astype(jnp.bfloat16)
    router = scatter_about(key_list[8], (SECTIONS, D, EXPERTS), D ** -0.5, 0.09375, ((0, 16),))
    gate_proj = scatter_about(key_list[9], (SECTIONS, D, EXPERTS * FF), D ** -0.5, 0.09375, ((0, 16), (2, 32)))
    up_proj = scatter_about(key_list[10], (SECTIONS, D, EXPERTS * FF), D ** -0.5, 0.09375, ((0, 16), (2, 32)))
    down_proj = scatter_about(key_list[11], (SECTIONS, EXPERTS * FF, D), FF ** -0.5, 0.1875, ((0, 16), (1, 32)))
    return dict(forward_in=forward_in, forward_new=forward_new, grad_in=grad_in, grad_new=grad_new, saved_inputs=saved_inputs, forward_ids=forward_ids, backward_ids=backward_ids, norm_gain=norm_gain, router=router, gate_proj=gate_proj, up_proj=up_proj, down_proj=down_proj)


routed_scale = 2.5
norm_eps = 1e-06

def norm_rows(inputs, gain):
    wide = inputs.astype(jnp.float32)
    inverse = lax.rsqrt(lax.optimization_barrier(jnp.mean(wide * wide, -1, keepdims=True)) + norm_eps)
    normed = (wide * inverse * gain.astype(jnp.float32)).astype(jnp.bfloat16)
    return (wide, inverse, normed)

def route_gates(normed, choices, router_cols):
    logits = jnp.dot(normed, router_cols, preferred_element_type=jnp.float32)
    onehot = (choices[:, :, None] == jnp.arange(router_cols.shape[1], dtype=jnp.int32)[None, None, :]).astype(jnp.float32)
    chosen = lax.optimization_barrier(jnp.sum(onehot * logits[:, None, :], -1))
    affin = jax.nn.sigmoid(chosen)
    total = lax.optimization_barrier(jnp.sum(affin, -1, keepdims=True))
    return (onehot, affin, total, routed_scale * affin / total)

def expert_forward(normed, gate_cols, up_cols, down_rows):
    pre_gate = jnp.dot(normed, gate_cols, preferred_element_type=jnp.float32)
    pre_up = jnp.dot(normed, up_cols, preferred_element_type=jnp.float32)
    active = (jax.nn.silu(pre_gate) * pre_up).astype(jnp.bfloat16)
    shards = N_EXPERT // EXPERTS
    width = active.shape[1] // shards
    summed = jnp.zeros((normed.shape[0], down_rows.shape[1]), jnp.float32)
    for shard in range(shards):
        piece = jnp.dot(active[:, shard * width:(shard + 1) * width], down_rows[shard * width:(shard + 1) * width], preferred_element_type=jnp.float32)
        summed = summed + piece.astype(jnp.bfloat16).astype(jnp.float32)
    return (pre_gate, pre_up, summed.astype(jnp.bfloat16))

def expert_backward(normed, cotangent, gate_cols, up_cols, down_rows):
    pre_gate, pre_up, output = expert_forward(normed, gate_cols, up_cols, down_rows)
    grad_act = jnp.dot(cotangent, down_rows.T, preferred_element_type=jnp.float32)
    sigma = jax.nn.sigmoid(pre_gate)
    grad_up = (grad_act * jax.nn.silu(pre_gate)).astype(jnp.bfloat16)
    grad_gate = (grad_act * pre_up * sigma * (1.0 + pre_gate * (1.0 - sigma))).astype(jnp.bfloat16)
    shards = N_EXPERT // EXPERTS
    width = grad_up.shape[1] // shards
    summed = jnp.zeros(normed.shape, jnp.float32)
    for shard in range(shards):
        cols = slice(shard * width, (shard + 1) * width)
        piece = jnp.dot(grad_gate[:, cols], gate_cols[:, cols].T, preferred_element_type=jnp.float32)
        piece = piece + jnp.dot(grad_up[:, cols], up_cols[:, cols].T, preferred_element_type=jnp.float32)
        summed = summed + piece.astype(jnp.bfloat16).astype(jnp.float32)
    return (output, summed.astype(jnp.bfloat16))

def layer_forward(inputs, choices, gain, router_cols, gate_all, up_all, down_all):
    wide, inverse, normed = norm_rows(inputs, gain)
    onehot, affin, total, gates = route_gates(normed, choices, router_cols)
    outputs = []
    for expert in range(EXPERTS):
        cols = slice(expert * FF, (expert + 1) * FF)
        outputs.append(expert_forward(normed, gate_all[:, cols], up_all[:, cols], down_all[cols])[2])
    stacked = jnp.stack(outputs).astype(jnp.float32)
    picked = jnp.einsum('tke,etd->tkd', onehot, stacked)
    return (wide + lax.optimization_barrier(jnp.sum(gates[:, :, None] * picked, 1))).astype(jnp.bfloat16)

def layer_backward(inputs, cotangent, choices, gain, router_cols, gate_all, up_all, down_all):
    wide, inverse, normed = norm_rows(inputs, gain)
    onehot, affin, total, gates = route_gates(normed, choices, router_cols)
    outputs = []
    grads = []
    for expert in range(EXPERTS):
        cols = slice(expert * FF, (expert + 1) * FF)
        output, grad_norm = expert_backward(normed, cotangent, gate_all[:, cols], up_all[:, cols], down_all[cols])
        outputs.append(output)
        grads.append(grad_norm)
    picked_out = jnp.einsum('tke,etd->tkd', onehot, jnp.stack(outputs).astype(jnp.float32))
    picked_grad = jnp.einsum('tke,etd->tkd', onehot, jnp.stack(grads).astype(jnp.float32))
    cot_wide = cotangent.astype(jnp.float32)
    grad_gates = lax.optimization_barrier(jnp.sum(cot_wide[:, None, :] * picked_out, -1))
    inner = lax.optimization_barrier(jnp.sum(gates * grad_gates, -1, keepdims=True))
    grad_affin = routed_scale / total * (grad_gates - inner / routed_scale)
    grad_logit = grad_affin * affin * (1.0 - affin)
    per_expert = lax.optimization_barrier(jnp.sum(grad_logit[:, :, None] * onehot, 1))
    grad_normed = lax.optimization_barrier(jnp.sum(gates[:, :, None] * picked_grad, 1))
    grad_normed = grad_normed + jnp.dot(per_expert, router_cols.astype(jnp.float32).T, precision=lax.Precision.HIGHEST)
    scaled = grad_normed * gain.astype(jnp.float32)
    result = cot_wide + inverse * scaled - wide * inverse ** 3 * lax.optimization_barrier(jnp.mean(scaled * wide, -1, keepdims=True))
    return result.astype(jnp.bfloat16)

def reference(forward_in, forward_new, grad_in, grad_new, saved_inputs, forward_ids, backward_ids, norm_gain, router, gate_proj, up_proj, down_proj):
    forward_all = jax.vmap(layer_forward)
    backward_all = jax.vmap(layer_backward)
    current = forward_in
    carried = grad_in
    forward_list = []
    backward_list = []
    for moment in range(MICRO):
        layer_outs = forward_all(current, forward_ids[moment], norm_gain, router, gate_proj, up_proj, down_proj)
        layer_grads = backward_all(saved_inputs[moment], carried, backward_ids[moment], norm_gain, router, gate_proj, up_proj, down_proj)
        forward_list.append(layer_outs)
        backward_list.append(layer_grads)
        if moment + 1 < MICRO:
            current = jnp.concatenate([forward_new[moment][None], layer_outs[:-1]], 0)
            carried = jnp.concatenate([layer_grads[1:], grad_new[moment][None]], 0)
    return (jnp.stack(forward_list), jnp.stack(backward_list))
```

```python
import jax
import jax.numpy as jnp
from jax import lax
from jax.sharding import PartitionSpec as P

MICRO = 2
CAP = 6


routed_scale = 2.5
norm_eps = 1e-06


def shifted(block, axis, distance):
    devices = range(lax.axis_size(axis))
    route = [(i - distance, i) for i in devices if i - distance in devices]
    return lax.ppermute(block, axis, route)


def norm_rows(inputs, gain):
    wide = inputs.astype(jnp.float32)
    inverse = lax.rsqrt(jnp.mean(wide * wide, -1, keepdims=True) + norm_eps)
    normed = (wide * inverse * gain.astype(jnp.float32)).astype(jnp.bfloat16)
    return (wide, inverse, normed)


def route_gates(normed, choices, router_cols):
    logits = jnp.dot(normed, router_cols, preferred_element_type=jnp.float32)
    onehot = (
        choices[:, :, None] == jnp.arange(router_cols.shape[1], dtype=jnp.int32)[None, None, :]
    ).astype(jnp.float32)
    chosen = jnp.sum(onehot * logits[:, None, :], -1)
    affin = jax.nn.sigmoid(chosen)
    total = jnp.sum(affin, -1, keepdims=True)
    return (onehot, affin, total, routed_scale * affin / total)


def slot_table(choices, experts):
    flat = choices.reshape(-1)
    member = (flat[:, None] == jnp.arange(experts, dtype=jnp.int32)[None, :]).astype(jnp.int32)
    entries = jnp.arange(flat.shape[0], dtype=jnp.int32)
    ahead = (entries[None, :] < entries[:, None]) & (flat[None, :] == flat[:, None])
    position = jnp.sum(ahead.astype(jnp.int32), 1)
    places = jnp.arange(CAP, dtype=jnp.int32)
    table = (position[None, None, :] == places[None, :, None]) & (member.T[:, None, :] == 1)
    return table.astype(jnp.bfloat16)


def expert_work(received, gate_cols, up_cols, down_rows):
    kinds, senders, items, width = received.shape
    normed = received[0].reshape(senders * items, width)
    pre_gate = jnp.dot(normed, gate_cols, preferred_element_type=jnp.float32)
    pre_up = jnp.dot(normed, up_cols, preferred_element_type=jnp.float32)
    active = (jax.nn.silu(pre_gate) * pre_up).astype(jnp.bfloat16)
    output = jnp.dot(active, down_rows, preferred_element_type=jnp.float32).astype(jnp.bfloat16)
    if kinds == 1:
        return output.reshape(1, senders, items, width)
    cotangent = received[1].reshape(senders * items, width)
    contract = (((1,), (1,)), ((), ()))
    grad_act = lax.dot_general(cotangent, down_rows, contract, preferred_element_type=jnp.float32)
    sigma = jax.nn.sigmoid(pre_gate)
    grad_up = (grad_act * jax.nn.silu(pre_gate)).astype(jnp.bfloat16)
    grad_gate = (grad_act * pre_up * sigma * (1.0 + pre_gate * (1.0 - sigma))).astype(jnp.bfloat16)
    grad_normed = lax.dot_general(
        grad_gate, gate_cols, contract, preferred_element_type=jnp.float32
    )
    grad_normed = grad_normed + lax.dot_general(
        grad_up, up_cols, contract, preferred_element_type=jnp.float32
    )
    stacked = jnp.stack([output, grad_normed.astype(jnp.bfloat16)])
    return stacked.reshape(2, senders, items, width)


def dispatch(payload, table, shards, gate_cols, up_cols, down_rows):
    kinds, count, width = payload.shape
    experts = table.shape[0]
    devices = experts * shards
    buffer = jnp.einsum("ecj,kjd->kecd", table, payload, preferred_element_type=jnp.float32).astype(
        jnp.bfloat16
    )
    sending = jnp.broadcast_to(buffer[:, :, None], (kinds, experts, shards, CAP, width)).reshape(
        kinds, devices, CAP, width
    )
    partial_sums = expert_work(
        lax.all_to_all(sending, "expert", split_axis=1, concat_axis=1, tiled=True),
        gate_cols,
        up_cols,
        down_rows,
    )
    returned = lax.all_to_all(partial_sums, "expert", split_axis=1, concat_axis=1, tiled=True)
    outs_kinds = returned.shape[0]
    results = jnp.sum(
        returned.reshape(outs_kinds, experts, shards, CAP, width).astype(jnp.float32), 2
    ).astype(jnp.bfloat16)
    return jnp.einsum("ecj,kecd->kjd", table, results, preferred_element_type=jnp.float32)


def section_forward(inputs, choices, gain, router_cols, gate_cols, up_cols, down_rows, shards):
    wide, inverse, normed = norm_rows(inputs, gain)
    onehot, affin, total, gates = route_gates(normed, choices, router_cols)
    tokens, picks = choices.shape
    table = slot_table(choices, router_cols.shape[1])
    payload = jnp.broadcast_to(normed[:, None, :], (tokens, picks, normed.shape[1])).reshape(
        1, tokens * picks, normed.shape[1]
    )
    picked = dispatch(payload, table, shards, gate_cols, up_cols, down_rows).reshape(
        tokens, picks, normed.shape[1]
    )
    return (wide + jnp.sum(gates[:, :, None] * picked, 1)).astype(jnp.bfloat16)


def section_backward(
    inputs, cotangent, choices, gain, router_cols, gate_cols, up_cols, down_rows, shards
):
    wide, inverse, normed = norm_rows(inputs, gain)
    onehot, affin, total, gates = route_gates(normed, choices, router_cols)
    tokens, picks = choices.shape
    width = normed.shape[1]
    table = slot_table(choices, router_cols.shape[1])
    both = jnp.stack([normed, cotangent])
    payload = jnp.broadcast_to(both[:, :, None, :], (2, tokens, picks, width)).reshape(
        2, tokens * picks, width
    )
    picked = dispatch(payload, table, shards, gate_cols, up_cols, down_rows).reshape(
        2, tokens, picks, width
    )
    cot_wide = cotangent.astype(jnp.float32)
    grad_gates = jnp.sum(cot_wide[:, None, :] * picked[0], -1)
    inner = jnp.sum(gates * grad_gates, -1, keepdims=True)
    grad_affin = routed_scale / total * (grad_gates - inner / routed_scale)
    grad_logit = grad_affin * affin * (1.0 - affin)
    per_expert = jnp.sum(grad_logit[:, :, None] * onehot, 1)
    grad_normed = jnp.sum(gates[:, :, None] * picked[1], 1)
    grad_normed = grad_normed + jnp.dot(
        per_expert, router_cols.astype(jnp.float32).T, precision=lax.Precision.HIGHEST
    )
    scaled = grad_normed * gain.astype(jnp.float32)
    result = (
        cot_wide + inverse * scaled - wide * inverse**3 * jnp.mean(scaled * wide, -1, keepdims=True)
    )
    return result.astype(jnp.bfloat16)


def per_device(
    forward_in,
    forward_new,
    grad_in,
    grad_new,
    saved_inputs,
    forward_ids,
    backward_ids,
    norm_gain,
    router,
    gate_proj,
    up_proj,
    down_proj,
):
    router_cols = router[0]
    shards = lax.axis_size("expert") // router_cols.shape[1]
    section_index = lax.axis_index("pipe")
    last_section = lax.axis_size("pipe") - 1
    gain = norm_gain[0]
    gate_cols = gate_proj[0]
    up_cols = up_proj[0]
    down_rows = down_proj[0]
    current = forward_in[0]
    carried = grad_in[0]
    forward_list = []
    backward_list = []
    for moment in range(MICRO):
        layer_outs = section_forward(
            current,
            forward_ids[moment, 0],
            gain,
            router_cols,
            gate_cols,
            up_cols,
            down_rows,
            shards,
        )
        layer_grads = section_backward(
            saved_inputs[moment, 0],
            carried,
            backward_ids[moment, 0],
            gain,
            router_cols,
            gate_cols,
            up_cols,
            down_rows,
            shards,
        )
        forward_list.append(layer_outs)
        backward_list.append(layer_grads)
        if moment + 1 < MICRO:
            arrived = shifted(layer_outs, "pipe", 1)
            current = jnp.where(section_index == 0, forward_new[moment], arrived)
            returned = shifted(layer_grads, "pipe", -1)
            carried = jnp.where(section_index == last_section, grad_new[moment], returned)
    return (jnp.stack(forward_list)[:, None], jnp.stack(backward_list)[:, None])


def solution(mesh):
    in_specs = (
        P("pipe", "expert", None),
        P(None, "expert", None),
        P("pipe", "expert", None),
        P(None, "expert", None),
        P(None, "pipe", "expert", None),
        P(None, "pipe", "expert", None),
        P(None, "pipe", "expert", None),
        P("pipe", None),
        P("pipe", None, None),
        P("pipe", None, "expert"),
        P("pipe", None, "expert"),
        P("pipe", "expert", None),
    )
    out_specs = (P(None, "pipe", "expert", None), P(None, "pipe", "expert", None))
    return jax.shard_map(
        per_device, mesh=mesh, in_specs=in_specs, out_specs=out_specs, check_vma=False
    )
```

```python
import functools

import jax
import jax.numpy as jnp
import numpy as np
from jax import lax
from jax.experimental import pallas as pl
from jax.experimental.pallas import tpu as pltpu
from jax.sharding import Mesh
from jax.sharding import PartitionSpec as P

CAP = 6
EXPERTS = 4
TOK = 8
CHIPS = 16
UNITS = 4
BLOCK = UNITS * CAP
ROWS = CHIPS * BLOCK
PACK = 128

routed_scale = 2.5
norm_eps = 1e-06
f32 = jnp.float32
bf16 = jnp.bfloat16

NT = (((1,), (1,)), ((), ()))


def dot(a, b):
    return jnp.dot(a, b, preferred_element_type=f32)


def dot_nt(a, b):
    return lax.dot_general(a, b, NT, preferred_element_type=f32)


def iota(shape, axis):
    return lax.broadcasted_iota(jnp.int32, shape, axis)


def whole(index, size):
    return jnp.floor((index.astype(f32) + 0.5) * (1.0 / size))


def row_codes(shape, axis):
    row = iota(shape, axis)
    expert = whole(row, ROWS // EXPERTS)
    offset = row.astype(f32) - BLOCK * whole(row, BLOCK)
    unit = jnp.floor((offset + 0.5) * (1.0 / CAP))
    return expert, unit, offset - CAP * unit


def tables(ids):
    cols = jnp.concatenate([u.astype(f32) for u in ids], 0)
    n = cols.shape[0]
    i, j = iota((n, n), 0), iota((n, n), 1)
    same = whole(i, TOK) == whole(j, TOK)
    col = [cols[:, k : k + 1] for k in range(2)]
    lane = [jnp.sum(jnp.where(i == j, c, 0.0), 0, keepdims=True) for c in col]
    col_pos, lane_pos = [], []
    for k in range(2):
        ahead = same & (j < i) & ((lane[0] == col[k]) | (lane[1] == col[k]))
        col_pos.append(jnp.sum(jnp.where(ahead, 1.0, 0.0), 1, keepdims=True))
        ahead = same & (i < j) & ((col[0] == lane[k]) | (col[1] == lane[k]))
        lane_pos.append(jnp.sum(jnp.where(ahead, 1.0, 0.0), 0, keepdims=True))
    return col, col_pos, lane, lane_pos


def dispatch(rows, ids):
    _, _, lane, lane_pos = tables(ids)
    shape = (ROWS, UNITS * TOK)
    expert, unit, slot = row_codes(shape, 0)
    hit = (expert == lane[0]) & (slot == lane_pos[0]) | (expert == lane[1]) & (slot == lane_pos[1])
    hit = hit & (unit == whole(iota(shape, 1), TOK))
    table = jnp.where(hit, 1.0, 0.0).astype(bf16)
    stacked = jnp.concatenate(rows, 0).astype(bf16)
    return dot(table, stacked).astype(bf16)


def norm_rows(wide, gain):
    inverse = lax.rsqrt(jnp.mean(wide * wide, -1, keepdims=True) + norm_eps)
    return inverse, (wide * inverse * gain).astype(bf16).astype(f32)


def route(normed, inverse, ids, router):
    logits = dot(normed.astype(bf16), router)
    lanes = iota(logits.shape, 1)
    affin = [
        jax.nn.sigmoid(jnp.sum(jnp.where(lanes == ids[:, k : k + 1], logits, 0.0), -1, keepdims=True))
        for k in range(2)
    ]
    at = iota((TOK, 128), 1)
    return jnp.where(at == 0, affin[0], jnp.where(at == 1, affin[1], inverse))


def prepare_kernel(x_ref, s_ref, c_ref, gain_ref, router_ref, fid_ref, bid_ref, out_ref, stat_ref):
    gain = gain_ref[...].astype(f32)
    router = router_ref[0]
    ids = [fid_ref[0, 0], bid_ref[0, 0], bid_ref[1, 0]]
    rows = []
    for n, wide in enumerate((x_ref[0], s_ref[0, 0], s_ref[1, 0])):
        inverse, normed = norm_rows(wide.astype(f32), gain)
        stat_ref[n] = route(normed, inverse, ids[n], router)
        rows.append(normed)
    units = [rows[0], rows[1], c_ref[0].astype(f32), rows[2]]
    out_ref[...] = dispatch(units, [ids[0], ids[1], ids[1], ids[2]])


def again_kernel(
    sec_ref, y_ref, fnew_ref, b_ref, gnew_ref, gain_ref, router_ref, fid_ref, bid_ref,
    out_ref, x_ref, c_ref, stat_ref, *, last,
):
    first = sec_ref[0, 0] == 0
    final = sec_ref[0, 0] == last
    x = jnp.where(first, fnew_ref[0].astype(f32), y_ref[...].astype(f32))
    c = jnp.where(final, gnew_ref[0].astype(f32), b_ref[...].astype(f32))
    x_ref[...] = x.astype(bf16)
    c_ref[...] = c.astype(bf16)
    ids = [fid_ref[1, 0], bid_ref[1, 0]]
    inverse, normed = norm_rows(x, gain_ref[...].astype(f32))
    stat_ref[...] = route(normed, inverse, ids[0], router_ref[0])
    half = x.shape[1] // 2
    units = [normed[:, :half], c[:, :half], normed[:, half:], c[:, half:]]
    out_ref[...] = dispatch(units, ids + ids)


def roll_up(value, count):
    return pltpu.roll(value, value.shape[0] - count, 0)


def experts(pre, grad_act, gu_ref, down_ref, out_ref):
    hidden = grad_act.shape[1]
    offset = iota((CHIPS, BLOCK, hidden), 1).reshape(ROWS, hidden)
    forward = offset < CAP
    backward = (offset >= CAP) & (offset < 2 * CAP)
    pre_gate, pre_up = pre[:, :hidden], pre[:, hidden:]
    sigma = jax.nn.sigmoid(pre_gate)
    silu = pre_gate * sigma
    active = silu * pre_up
    dg = jnp.sum(jnp.where(backward, active.astype(bf16).astype(f32) * grad_act, 0.0), 1, keepdims=True)
    grad_up = grad_act * silu
    grad_gate = grad_act * pre_up * sigma * (1.0 + pre_gate * (1.0 - sigma))
    parts = [
        jnp.where(forward, active, 0.0),
        jnp.where(backward, grad_gate, 0.0),
        jnp.where(backward, grad_up, 0.0),
    ]
    parts = [(p + pltpu.roll(p, 2 * CAP, 0)).astype(bf16) for p in parts]
    grads = jnp.concatenate(parts[1:], 1)
    width = down_ref.shape[1] // 2
    step = 256
    left = iota((CHIPS, BLOCK, step), 1).reshape(ROWS, step) < 2 * CAP
    for n in range(0, width, step):
        sides = []
        for at in (n, n + width):
            side = dot(parts[0], down_ref[:, at : at + step])
            sides.append(side + dot_nt(grads, gu_ref[at : at + step, :]))
        out_ref[:, n : n + step] = jnp.where(left, sides[0], sides[1]).astype(bf16)
    high = dg.astype(bf16).astype(f32)
    low = pltpu.roll(jnp.broadcast_to(dg - high, (ROWS, PACK)), 2 * CAP, 0)
    high = jnp.broadcast_to(high, (ROWS, PACK))
    out_ref[:, width : width + PACK] = jnp.where(left[:, :PACK], high, low).astype(bf16)


def experts_first_kernel(in_ref, gu_ref, down_ref, out_ref, keep_ref):
    pre = dot(in_ref[...], gu_ref[...])
    grad_act = roll_up(dot_nt(in_ref[...], down_ref[...]), CAP)
    keep_ref[...] = roll_up(pre, 2 * CAP)
    experts(pre, grad_act, gu_ref, down_ref, out_ref)


def experts_second_kernel(in_ref, keep_ref, gu_ref, down_ref, out_ref):
    width = in_ref.shape[1]
    rows = in_ref[...]
    pre = dot(rows, gu_ref[:width, :]) + roll_up(dot(rows, gu_ref[width:, :]), 2 * CAP)
    grad_act = dot_nt(rows, down_ref[:, :width]) + roll_up(dot_nt(rows, down_ref[:, width:]), 2 * CAP)
    offset = iota((CHIPS, BLOCK, pre.shape[1]), 1).reshape(pre.shape)
    pre = jnp.where(offset < CAP, pre, keep_ref[...])
    experts(pre, grad_act, gu_ref, down_ref, out_ref)


def combine(in_ref, x, s, cot, x_stat, s_stat, fid, bid, gain, router_rows):
    col, col_pos, _, _ = tables([fid, bid])
    shape = (TOK, ROWS)
    expert, unit, slot = row_codes(shape, 1)
    blocks = []
    for h in range(2):
        for u in range(2):
            at = slice(u * TOK, (u + 1) * TOK)
            for k in range(2):
                hit = (expert == col[k][at]) & (slot == col_pos[k][at]) & (unit == 2 * h + u)
                blocks.append(jnp.where(hit, 1.0, 0.0))
    table = jnp.concatenate(blocks, 0).astype(bf16)
    picked = dot(table, in_ref[...])
    width = x.shape[1] // 2

    def taken(u, k):
        rows = [picked[((h * 2 + u) * 2 + k) * TOK :][:TOK] for h in range(2)]
        value = jnp.concatenate([r[:, :width] for r in rows], 1)
        return value, rows[0][:, width : width + 1] + rows[1][:, width : width + 1]

    def gates(stat):
        affin = [stat[:, 0:1], stat[:, 1:2]]
        total = affin[0] + affin[1]
        return affin, total, [routed_scale * a / total for a in affin]

    _, _, g = gates(x_stat)
    layer_out = x + (g[0] * taken(0, 0)[0] + g[1] * taken(0, 1)[0])
    affin, total, g = gates(s_stat)
    inverse = s_stat[:, 2:3]
    back0, dg0 = taken(1, 0)
    back1, dg1 = taken(1, 1)
    inner = g[0] * dg0 + g[1] * dg1
    grad_normed = g[0] * back0 + g[1] * back1
    grad_logit = [
        routed_scale / total * (dg - inner / routed_scale) * a * (1.0 - a)
        for dg, a in zip((dg0, dg1), affin)
    ]
    for e in range(EXPERTS):
        share = jnp.where(bid[:, 0:1] == e, grad_logit[0], 0.0)
        share = share + jnp.where(bid[:, 1:2] == e, grad_logit[1], 0.0)
        grad_normed = grad_normed + share * router_rows[e : e + 1]
    scaled = grad_normed * gain
    mean = jnp.mean(scaled * s, -1, keepdims=True)
    grad = cot + inverse * scaled - s * inverse * inverse * inverse * mean
    return layer_out.astype(bf16), grad.astype(bf16)


def combine_first_kernel(
    in_ref, x_ref, s_ref, c_ref, stat_ref, fid_ref, bid_ref, gain_ref, router_ref, y_ref, b_ref
):
    y, b = combine(
        in_ref, x_ref[0].astype(f32), s_ref[0, 0].astype(f32), c_ref[0].astype(f32),
        stat_ref[0], stat_ref[1], fid_ref[0, 0], bid_ref[0, 0],
        gain_ref[...].astype(f32), router_ref[...],
    )
    y_ref[...] = y
    b_ref[...] = b


def combine_second_kernel(
    in_ref, x_ref, s_ref, c_ref, stat_ref, x_stat_ref, fid_ref, bid_ref, gain_ref, router_ref,
    y0_ref, b0_ref, y_ref, b_ref,
):
    y, b = combine(
        in_ref, x_ref[...].astype(f32), s_ref[1, 0].astype(f32), c_ref[...].astype(f32),
        x_stat_ref[...], stat_ref[2], fid_ref[1, 0], bid_ref[1, 0],
        gain_ref[...].astype(f32), router_ref[...],
    )
    y_ref[0, 0] = y0_ref[...]
    b_ref[0, 0] = b0_ref[...]
    y_ref[1, 0] = y
    b_ref[1, 0] = b


def call(kernel, outs, *args, smem=0):
    spec = pl.BlockSpec(memory_space=pltpu.VMEM)
    first = pl.BlockSpec(memory_space=pltpu.SMEM)
    outs = [jax.ShapeDtypeStruct(*o) for o in outs]
    return pl.pallas_call(
        kernel,
        out_shape=outs,
        in_specs=[first] * smem + [spec] * (len(args) - smem),
        out_specs=[spec] * len(outs),
        compiler_params=pltpu.CompilerParams(vmem_limit_bytes=48 * 2**20),
    )(*args)


def swapped(block):
    return lax.ppermute(block, "core", [(0, 1), (1, 0)])


def exchanged(block):
    return lax.all_to_all(block, ("x", "y"), split_axis=0, concat_axis=0, tiled=True)


def shifted(block, distance):
    count = lax.axis_size("pipe")
    route_ = [(i - distance, i) for i in range(count) if 0 <= i - distance < count]
    return lax.ppermute(block, "pipe", route_)


def per_device(
    forward_in, forward_new, grad_in, grad_new, saved_inputs, forward_ids, backward_ids,
    norm_gain, router, gate_proj, up_proj, down_proj,
):
    width = forward_in.shape[-1]
    row = (TOK, width)
    stat = (TOK, 128)
    sent, stats = call(
        prepare_kernel,
        [((ROWS, width), bf16), ((3, *stat), f32)],
        forward_in, saved_inputs, grad_in, norm_gain, router, forward_ids, backward_ids,
    )
    gates_, ups, downs = gate_proj[0], up_proj[0], down_proj[0]
    gate_up = jnp.concatenate([gates_, swapped(gates_), ups, swapped(ups)], 1)
    down = jnp.concatenate([downs, swapped(downs)], 0)
    router_rows = router[0].T.astype(f32)
    hidden = gate_up.shape[1]
    packed = (ROWS, width // 2 + PACK)

    came = exchanged(sent)
    sent, keep = call(
        experts_first_kernel, [(packed, bf16), ((ROWS, hidden), f32)], came, gate_up, down
    )
    came = exchanged(sent)
    y0, b0 = call(
        combine_first_kernel, [(row, bf16)] * 2,
        came, forward_in, saved_inputs, grad_in, stats, forward_ids, backward_ids, norm_gain, router_rows,
    )
    section = lax.axis_index("pipe").astype(jnp.int32).reshape(1, 1)
    sent, x1, c1, x1_stat = call(
        functools.partial(again_kernel, last=lax.axis_size("pipe") - 1),
        [((ROWS, width // 2), bf16), (row, bf16), (row, bf16), (stat, f32)],
        section, shifted(y0, 1), forward_new, shifted(b0, -1), grad_new, norm_gain, router,
        forward_ids, backward_ids,
        smem=1,
    )
    came = exchanged(sent)
    (sent,) = call(experts_second_kernel, [(packed, bf16)], came, keep, gate_up, down)
    came = exchanged(sent)
    full = (2, 1, *row)
    return tuple(
        call(
            combine_second_kernel, [(full, bf16)] * 2,
            came, x1, saved_inputs, c1, stats, x1_stat, forward_ids, backward_ids, norm_gain, router_rows,
            y0, b0,
        )
    )


def solution(mesh):
    split = Mesh(np.asarray(mesh.devices).reshape(-1, 4, 4, 2), ("pipe", "x", "y", "core"))
    tokens = ("x", "y", "core")
    in_specs = (
        P("pipe", tokens, None),
        P(None, tokens, None),
        P("pipe", tokens, None),
        P(None, tokens, None),
        P(None, "pipe", tokens, None),
        P(None, "pipe", tokens, None),
        P(None, "pipe", tokens, None),
        P("pipe", None),
        P("pipe", None, None),
        P("pipe", None, tokens),
        P("pipe", None, tokens),
        P("pipe", tokens, None),
    )
    out_specs = (P(None, "pipe", tokens, None), P(None, "pipe", tokens, None))
    return jax.shard_map(
        per_device, mesh=split, in_specs=in_specs, out_specs=out_specs, check_vma=False
    )
```

```python
import functools

import jax
import jax.numpy as jnp
import numpy as np
from jax import lax
from jax.experimental import pallas as pl
from jax.experimental.pallas import tpu as pltpu
from jax.sharding import Mesh
from jax.sharding import PartitionSpec as P

CAP = 6
EXPERTS = 4
TOK = 8
CHIPS = 16
UNITS = 4
BLOCK = UNITS * CAP
ROWS = CHIPS * BLOCK
PACK = 128

routed_scale = 2.5
norm_eps = 1e-06
f32 = jnp.float32
bf16 = jnp.bfloat16

NT = (((1,), (1,)), ((), ()))


def dot(a, b):
    return jnp.dot(a, b, preferred_element_type=f32)


def dot_nt(a, b):
    return lax.dot_general(a, b, NT, preferred_element_type=f32)


def iota(shape, axis):
    return lax.broadcasted_iota(jnp.int32, shape, axis)


def whole(index, size):
    return jnp.floor((index.astype(f32) + 0.5) * (1.0 / size))


def row_codes(shape, axis):
    row = iota(shape, axis)
    expert = whole(row, ROWS // EXPERTS)
    offset = row.astype(f32) - BLOCK * whole(row, BLOCK)
    unit = jnp.floor((offset + 0.5) * (1.0 / CAP))
    return expert, unit, offset - CAP * unit


def columns(ids):
    wide = ids.astype(f32)
    here = iota((TOK, TOK), 0) == iota((TOK, TOK), 1)
    return [jnp.sum(jnp.where(here, wide[k : k + 1], 0.0), 1, keepdims=True) for k in range(2)]


def tables(choices):
    col = [jnp.concatenate([c[k] for c in choices], 0) for k in range(2)]
    n = col[0].shape[0]
    i, j = iota((n, n), 0), iota((n, n), 1)
    same = whole(i, TOK) == whole(j, TOK)
    lane = [jnp.sum(jnp.where(i == j, c, 0.0), 0, keepdims=True) for c in col]
    col_pos, lane_pos = [], []
    for k in range(2):
        ahead = same & (j < i) & ((lane[0] == col[k]) | (lane[1] == col[k]))
        col_pos.append(jnp.sum(jnp.where(ahead, 1.0, 0.0), 1, keepdims=True))
        ahead = same & (i < j) & ((col[0] == lane[k]) | (col[1] == lane[k]))
        lane_pos.append(jnp.sum(jnp.where(ahead, 1.0, 0.0), 0, keepdims=True))
    return col, col_pos, lane, lane_pos


def dispatch_table(choices):
    _, _, lane, lane_pos = tables(choices)
    shape = (ROWS, UNITS * TOK)
    expert, unit, slot = row_codes(shape, 0)
    hit = (expert == lane[0]) & (slot == lane_pos[0]) | (expert == lane[1]) & (slot == lane_pos[1])
    hit = hit & (unit == whole(iota(shape, 1), TOK))
    return jnp.where(hit, 1.0, 0.0)


def norm_rows(wide, gain):
    inverse = lax.rsqrt(jnp.mean(wide * wide, -1, keepdims=True) + norm_eps)
    return inverse, (wide * inverse * gain).astype(bf16).astype(f32)


def route(normed, inverse, choice, router):
    logits = dot_nt(normed.astype(bf16), router)
    lanes = iota(logits.shape, 1).astype(f32)
    affin = [
        jax.nn.sigmoid(jnp.sum(jnp.where(lanes == choice[k], logits, 0.0), -1, keepdims=True))
        for k in range(2)
    ]
    at = iota((TOK, 128), 1)
    return jnp.where(at == 0, affin[0], jnp.where(at == 1, affin[1], inverse))


def prepare_kernel(
    x_hbm, s_hbm, c_hbm, gain_hbm, router_hbm, fid_hbm, bid_hbm, out_hbm, stat_ref,
    x_ref, s_ref, c_ref, gain_ref, router_ref, fid_ref, bid_ref, out_ref, in_sem, out_sem,
):
    sources = (fid_hbm, bid_hbm, x_hbm, s_hbm, gain_hbm, router_hbm, c_hbm)
    places = (fid_ref, bid_ref, x_ref, s_ref, gain_ref, router_ref, c_ref)
    fetches = [pltpu.make_async_copy(a, b, in_sem.at[n]) for n, (a, b) in enumerate(zip(sources, places))]
    for fetch in fetches:
        fetch.start()
    fetches[0].wait()
    fetches[1].wait()
    choices = [columns(ids) for ids in (fid_ref[0, 0], bid_ref[0, 0], bid_ref[1, 0])]
    table = dispatch_table([choices[0], choices[1], choices[1], choices[2]])
    for fetch in fetches[2:]:
        fetch.wait()
    gain = gain_ref[...].astype(f32)
    rows = []
    for n, wide in enumerate((x_ref[0], s_ref[0, 0], s_ref[1, 0])):
        inverse, normed = norm_rows(wide.astype(f32), gain)
        stat_ref[n] = route(normed, inverse, choices[n], router_ref[...])
        rows.append(normed)
    stacked = jnp.concatenate([rows[0], rows[1], c_ref[0].astype(f32), rows[2]], 0).astype(bf16)
    step = ROWS // EXPERTS
    sends = []
    for e in range(EXPERTS):
        at = pl.ds(e * step, step)
        out_ref[at] = dot(table[e * step : (e + 1) * step].astype(bf16), stacked).astype(bf16)
        sends.append(pltpu.make_async_copy(out_ref.at[at], out_hbm.at[at], out_sem.at[e]))
        sends[-1].start()
    for send in sends:
        send.wait()


def again_kernel(
    sec_ref, y_ref, fnew_ref, b_ref, gnew_ref, gain_ref, router_ref, fid_ref, bid_ref,
    out_ref, x_ref, c_ref, stat_ref, *, last,
):
    first = sec_ref[0, 0] == 0
    final = sec_ref[0, 0] == last
    x = jnp.where(first, fnew_ref[0].astype(f32), y_ref[...].astype(f32))
    c = jnp.where(final, gnew_ref[0].astype(f32), b_ref[...].astype(f32))
    x_ref[...] = x.astype(bf16)
    c_ref[...] = c.astype(bf16)
    choices = [columns(fid_ref[1, 0]), columns(bid_ref[1, 0])]
    inverse, normed = norm_rows(x, gain_ref[...].astype(f32))
    stat_ref[...] = route(normed, inverse, choices[0], router_ref[...])
    half = x.shape[1] // 2
    units = [normed[:, :half], c[:, :half], normed[:, half:], c[:, half:]]
    table = dispatch_table(choices + choices).astype(bf16)
    out_ref[...] = dot(table, jnp.concatenate(units, 0).astype(bf16)).astype(bf16)


def roll_up(value, count):
    return pltpu.roll(value, value.shape[0] - count, 0)


def experts(pre, grad_act, gu_ref, down_ref, out_ref):
    hidden = grad_act.shape[1]
    offset = iota((CHIPS, BLOCK, hidden), 1).reshape(ROWS, hidden)
    forward = offset < CAP
    backward = (offset >= CAP) & (offset < 2 * CAP)
    pre_gate, pre_up = pre[:, :hidden], pre[:, hidden:]
    sigma = jax.nn.sigmoid(pre_gate)
    silu = pre_gate * sigma
    active = silu * pre_up
    dg = jnp.sum(jnp.where(backward, active.astype(bf16).astype(f32) * grad_act, 0.0), 1, keepdims=True)
    grad_up = grad_act * silu
    grad_gate = grad_act * pre_up * sigma * (1.0 + pre_gate * (1.0 - sigma))
    parts = [
        jnp.where(forward, active, 0.0),
        jnp.where(backward, grad_gate, 0.0),
        jnp.where(backward, grad_up, 0.0),
    ]
    parts = [(p + pltpu.roll(p, 2 * CAP, 0)).astype(bf16) for p in parts]
    grads = jnp.concatenate(parts[1:], 1)
    width = down_ref.shape[1] // 2
    step = 256
    left = iota((CHIPS, BLOCK, step), 1).reshape(ROWS, step) < 2 * CAP
    for n in range(0, width, step):
        sides = []
        for at in (n, n + width):
            side = dot(parts[0], down_ref[:, at : at + step])
            sides.append(side + dot_nt(grads, gu_ref[at : at + step, :]))
        out_ref[:, n : n + step] = jnp.where(left, sides[0], sides[1]).astype(bf16)
    high = dg.astype(bf16).astype(f32)
    low = pltpu.roll(jnp.broadcast_to(dg - high, (ROWS, PACK)), 2 * CAP, 0)
    high = jnp.broadcast_to(high, (ROWS, PACK))
    out_ref[:, width : width + PACK] = jnp.where(left[:, :PACK], high, low).astype(bf16)


CHUNKS = 4


class Weights:
    def __init__(self, w_hbm, gu_ref, down_ref, sems):
        depth, width = w_hbm[0].shape[1:]
        self.chunk = depth // CHUNKS
        self.groups = []
        for n in range(CHUNKS):
            at = pl.ds(n * self.chunk, self.chunk)
            self.groups.append(
                [
                    pltpu.make_async_copy(
                        w_hbm[i].at[0, at, :], gu_ref.at[at, i * width : (i + 1) * width], sems.at[n * 4 + i]
                    )
                    for i in range(4)
                ]
            )
        self.groups.append(
            [
                pltpu.make_async_copy(
                    w_hbm[4 + i].at[0], down_ref.at[i * width : (i + 1) * width, :], sems.at[CHUNKS * 4 + i]
                )
                for i in range(2)
            ]
        )
        self.start(0)
        self.start(1)

    def start(self, n):
        if n < len(self.groups):
            for copy in self.groups[n]:
                copy.start()

    def wait(self, n):
        for copy in self.groups[n]:
            copy.wait()
        self.start(n + 2)


def experts_first_kernel(in_ref, *refs):
    w_hbm, (out_ref, keep_ref, gu_ref, down_ref, sems) = refs[:6], refs[6:]
    weights = Weights(w_hbm, gu_ref, down_ref, sems)
    pre = 0.0
    for n in range(CHUNKS):
        weights.wait(n)
        at = slice(n * weights.chunk, (n + 1) * weights.chunk)
        pre = pre + dot(in_ref[:, at], gu_ref[at, :])
    keep_ref[...] = roll_up(pre, 2 * CAP)
    weights.wait(CHUNKS)
    grad_act = roll_up(dot_nt(in_ref[...], down_ref[...]), CAP)
    experts(pre, grad_act, gu_ref, down_ref, out_ref)


def experts_second_kernel(in_ref, keep_ref, *refs):
    w_hbm, (out_ref, gu_ref, down_ref, sems) = refs[:6], refs[6:]
    weights = Weights(w_hbm, gu_ref, down_ref, sems)
    width = in_ref.shape[1]
    sides = [0.0, 0.0]
    for n in range(CHUNKS):
        weights.wait(n)
        h, at = divmod(n * weights.chunk, width)
        part = dot(in_ref[:, at : at + weights.chunk], gu_ref[n * weights.chunk : (n + 1) * weights.chunk, :])
        sides[h] = sides[h] + part
    pre = sides[0] + roll_up(sides[1], 2 * CAP)
    weights.wait(CHUNKS)
    rows = in_ref[...]
    grad_act = dot_nt(rows, down_ref[:, :width]) + roll_up(dot_nt(rows, down_ref[:, width:]), 2 * CAP)
    offset = iota((CHIPS, BLOCK, pre.shape[1]), 1).reshape(pre.shape)
    pre = jnp.where(offset < CAP, pre, keep_ref[...])
    experts(pre, grad_act, gu_ref, down_ref, out_ref)


def combine(in_ref, x, s, cot, x_stat, s_stat, fid, bid, gain, router_rows):
    choices = [columns(fid), columns(bid)]
    col, col_pos, _, _ = tables(choices)
    shape = (TOK, ROWS)
    expert, unit, slot = row_codes(shape, 1)
    blocks = []
    for h in range(2):
        for u in range(2):
            at = slice(u * TOK, (u + 1) * TOK)
            for k in range(2):
                hit = (expert == col[k][at]) & (slot == col_pos[k][at]) & (unit == 2 * h + u)
                blocks.append(jnp.where(hit, 1.0, 0.0))
    table = jnp.concatenate(blocks, 0).astype(bf16)
    picked = dot(table, in_ref[...])
    width = x.shape[1] // 2

    def taken(u, k):
        rows = [picked[((h * 2 + u) * 2 + k) * TOK :][:TOK] for h in range(2)]
        value = jnp.concatenate([r[:, :width] for r in rows], 1)
        return value, rows[0][:, width : width + 1] + rows[1][:, width : width + 1]

    def gates(stat):
        affin = [stat[:, 0:1], stat[:, 1:2]]
        total = affin[0] + affin[1]
        return affin, total, [routed_scale * a / total for a in affin]

    _, _, g = gates(x_stat)
    layer_out = x + (g[0] * taken(0, 0)[0] + g[1] * taken(0, 1)[0])
    affin, total, g = gates(s_stat)
    inverse = s_stat[:, 2:3]
    back0, dg0 = taken(1, 0)
    back1, dg1 = taken(1, 1)
    inner = g[0] * dg0 + g[1] * dg1
    grad_normed = g[0] * back0 + g[1] * back1
    grad_logit = [
        routed_scale / total * (dg - inner / routed_scale) * a * (1.0 - a)
        for dg, a in zip((dg0, dg1), affin)
    ]
    for e in range(EXPERTS):
        share = jnp.where(choices[1][0] == e, grad_logit[0], 0.0)
        share = share + jnp.where(choices[1][1] == e, grad_logit[1], 0.0)
        grad_normed = grad_normed + share * router_rows[e : e + 1].astype(f32)
    scaled = grad_normed * gain
    mean = jnp.mean(scaled * s, -1, keepdims=True)
    grad = cot + inverse * scaled - s * inverse * inverse * inverse * mean
    return layer_out.astype(bf16), grad.astype(bf16)


def combine_first_kernel(
    in_ref, x_ref, s_ref, c_ref, stat_ref, fid_ref, bid_ref, gain_ref, router_ref, y_ref, b_ref
):
    y, b = combine(
        in_ref, x_ref[0].astype(f32), s_ref[0, 0].astype(f32), c_ref[0].astype(f32),
        stat_ref[0], stat_ref[1], fid_ref[0, 0], bid_ref[0, 0],
        gain_ref[...].astype(f32), router_ref[...],
    )
    y_ref[...] = y
    b_ref[...] = b


def combine_second_kernel(
    in_ref, x_ref, s_ref, c_ref, stat_ref, x_stat_ref, fid_ref, bid_ref, gain_ref, router_ref,
    y0_ref, b0_ref, y_ref, b_ref,
):
    y, b = combine(
        in_ref, x_ref[...].astype(f32), s_ref[1, 0].astype(f32), c_ref[...].astype(f32),
        x_stat_ref[...], stat_ref[2], fid_ref[1, 0], bid_ref[1, 0],
        gain_ref[...].astype(f32), router_ref[...],
    )
    y_ref[0, 0] = y0_ref[...]
    b_ref[0, 0] = b0_ref[...]
    y_ref[1, 0] = y
    b_ref[1, 0] = b


VMEM_BYTES = 28 * 2**20
PREPARE_BYTES = 62 * 2**20


def in_hbm(args):
    return [pltpu.with_memory_space_constraint(a, pltpu.HBM) for a in args]


def call(kernel, outs, *args, smem=0, weights=()):
    spec = pl.BlockSpec(memory_space=pltpu.VMEM)
    first = pl.BlockSpec(memory_space=pltpu.SMEM)
    far = pl.BlockSpec(memory_space=pltpu.HBM)
    outs = [jax.ShapeDtypeStruct(*o) for o in outs]
    scratch = []
    if weights:
        depth, width = weights[0].shape[1:]
        scratch = [
            pltpu.VMEM((depth, 4 * width), bf16),
            pltpu.VMEM((2 * width, depth), bf16),
            pltpu.SemaphoreType.DMA((CHUNKS * 4 + 2,)),
        ]
    return pl.pallas_call(
        kernel,
        out_shape=outs,
        in_specs=[first] * smem + [spec] * (len(args) - smem) + [far] * len(weights),
        out_specs=[spec] * len(outs),
        scratch_shapes=scratch,
        compiler_params=pltpu.CompilerParams(vmem_limit_bytes=VMEM_BYTES),
    )(*args, *in_hbm(weights))


def swapped(block):
    return lax.ppermute(block, "core", [(0, 1), (1, 0)])


def exchanged(block):
    return lax.all_to_all(block, ("x", "y"), split_axis=0, concat_axis=0, tiled=True)


def shifted(block, distance):
    count = lax.axis_size("pipe")
    route_ = [(i - distance, i) for i in range(count) if 0 <= i - distance < count]
    return lax.ppermute(block, "pipe", route_)


def per_device(
    forward_in, forward_new, grad_in, grad_new, saved_inputs, forward_ids, backward_ids,
    norm_gain, router, gate_proj, up_proj, down_proj,
):
    width = forward_in.shape[-1]
    row = (TOK, width)
    stat = (TOK, 128)
    forward_ids = forward_ids.transpose(0, 1, 3, 2)
    backward_ids = backward_ids.transpose(0, 1, 3, 2)
    router = router[0].T
    args = (forward_in, saved_inputs, grad_in, norm_gain, router, forward_ids, backward_ids)
    sent, stats = pl.pallas_call(
        prepare_kernel,
        out_shape=[jax.ShapeDtypeStruct((ROWS, width), bf16), jax.ShapeDtypeStruct((3, *stat), f32)],
        in_specs=[pl.BlockSpec(memory_space=pltpu.HBM)] * len(args),
        out_specs=[pl.BlockSpec(memory_space=pltpu.HBM), pl.BlockSpec(memory_space=pltpu.VMEM)],
        scratch_shapes=[pltpu.VMEM(a.shape, a.dtype) for a in args]
        + [
            pltpu.VMEM((ROWS, width), bf16),
            pltpu.SemaphoreType.DMA((len(args),)),
            pltpu.SemaphoreType.DMA((EXPERTS,)),
        ],
        compiler_params=pltpu.CompilerParams(vmem_limit_bytes=PREPARE_BYTES),
    )(*in_hbm(args))
    weights = []
    for own in (gate_proj, up_proj, down_proj):
        weights += [own, swapped(own)]
    hidden = 4 * gate_proj.shape[-1]
    packed = (ROWS, width // 2 + PACK)

    came = exchanged(sent)
    sent, keep = call(
        experts_first_kernel, [(packed, bf16), ((ROWS, hidden), f32)], came, weights=weights
    )
    came = exchanged(sent)
    y0, b0 = call(
        combine_first_kernel, [(row, bf16)] * 2,
        came, forward_in, saved_inputs, grad_in, stats, forward_ids, backward_ids, norm_gain, router,
    )
    section = lax.axis_index("pipe").astype(jnp.int32).reshape(1, 1)
    sent, x1, c1, x1_stat = call(
        functools.partial(again_kernel, last=lax.axis_size("pipe") - 1),
        [((ROWS, width // 2), bf16), (row, bf16), (row, bf16), (stat, f32)],
        section, shifted(y0, 1), forward_new, shifted(b0, -1), grad_new, norm_gain, router,
        forward_ids, backward_ids,
        smem=1,
    )
    came = exchanged(sent)
    (sent,) = call(experts_second_kernel, [(packed, bf16)], came, keep, weights=weights)
    came = exchanged(sent)
    full = (2, 1, *row)
    return tuple(
        call(
            combine_second_kernel, [(full, bf16)] * 2,
            came, x1, saved_inputs, c1, stats, x1_stat, forward_ids, backward_ids, norm_gain, router,
            y0, b0,
        )
    )


def solution(mesh):
    split = Mesh(np.asarray(mesh.devices).reshape(-1, 4, 4, 2), ("pipe", "x", "y", "core"))
    tokens = ("x", "y", "core")
    in_specs = (
        P("pipe", tokens, None),
        P(None, tokens, None),
        P("pipe", tokens, None),
        P(None, tokens, None),
        P(None, "pipe", tokens, None),
        P(None, "pipe", tokens, None),
        P(None, "pipe", tokens, None),
        P("pipe", None),
        P("pipe", None, None),
        P("pipe", None, tokens),
        P("pipe", None, tokens),
        P("pipe", tokens, None),
    )
    out_specs = (P(None, "pipe", tokens, None), P(None, "pipe", tokens, None))
    return jax.shard_map(
        per_device, mesh=split, in_specs=in_specs, out_specs=out_specs, check_vma=False
    )
```

```python
import functools

import jax
import jax.numpy as jnp
import numpy as np
from jax import lax
from jax.experimental import pallas as pl
from jax.experimental.pallas import tpu as pltpu
from jax.sharding import Mesh
from jax.sharding import PartitionSpec as P

CAP = 6
EXPERTS = 4
TOK = 8
CHIPS = 16
UNITS = 4
BLOCK = UNITS * CAP
ROWS = CHIPS * BLOCK
PACK = 128

routed_scale = 2.5
norm_eps = 1e-06
f32 = jnp.float32
bf16 = jnp.bfloat16

NT = (((1,), (1,)), ((), ()))


def dot(a, b):
    return jnp.dot(a, b, preferred_element_type=f32)


def dot_nt(a, b):
    return lax.dot_general(a, b, NT, preferred_element_type=f32)


def iota(shape, axis):
    return lax.broadcasted_iota(jnp.int32, shape, axis)


def whole(index, size):
    return jnp.floor((index.astype(f32) + 0.5) * (1.0 / size))


def row_codes(shape, axis):
    row = iota(shape, axis)
    expert = whole(row, ROWS // EXPERTS)
    offset = row.astype(f32) - BLOCK * whole(row, BLOCK)
    unit = jnp.floor((offset + 0.5) * (1.0 / CAP))
    return expert, unit, offset - CAP * unit


def columns(ids):
    wide = ids.astype(f32)
    here = iota((TOK, TOK), 0) == iota((TOK, TOK), 1)
    return [jnp.sum(jnp.where(here, wide[k : k + 1], 0.0), 1, keepdims=True) for k in range(2)]


def tables(choices):
    col = [jnp.concatenate([c[k] for c in choices], 0) for k in range(2)]
    n = col[0].shape[0]
    i, j = iota((n, n), 0), iota((n, n), 1)
    same = whole(i, TOK) == whole(j, TOK)
    lane = [jnp.sum(jnp.where(i == j, c, 0.0), 0, keepdims=True) for c in col]
    col_pos, lane_pos = [], []
    for k in range(2):
        ahead = same & (j < i) & ((lane[0] == col[k]) | (lane[1] == col[k]))
        col_pos.append(jnp.sum(jnp.where(ahead, 1.0, 0.0), 1, keepdims=True))
        ahead = same & (i < j) & ((col[0] == lane[k]) | (col[1] == lane[k]))
        lane_pos.append(jnp.sum(jnp.where(ahead, 1.0, 0.0), 0, keepdims=True))
    return col, col_pos, lane, lane_pos


def dispatch_table(choices):
    _, _, lane, lane_pos = tables(choices)
    shape = (ROWS, UNITS * TOK)
    expert, unit, slot = row_codes(shape, 0)
    hit = (expert == lane[0]) & (slot == lane_pos[0]) | (expert == lane[1]) & (slot == lane_pos[1])
    hit = hit & (unit == whole(iota(shape, 1), TOK))
    return jnp.where(hit, 1.0, 0.0)


def norm_rows(wide, gain):
    inverse = lax.rsqrt(jnp.mean(wide * wide, -1, keepdims=True) + norm_eps)
    return inverse, (wide * inverse * gain).astype(bf16).astype(f32)


def route(normed, inverse, choice, router):
    logits = dot_nt(normed.astype(bf16), router)
    lanes = iota(logits.shape, 1).astype(f32)
    affin = [
        jax.nn.sigmoid(jnp.sum(jnp.where(lanes == choice[k], logits, 0.0), -1, keepdims=True))
        for k in range(2)
    ]
    at = iota((TOK, 128), 1)
    return jnp.where(at == 0, affin[0], jnp.where(at == 1, affin[1], inverse))


def prepare_kernel(
    x_hbm, s_hbm, c_hbm, gain_hbm, router_hbm, fid_hbm, bid_hbm, out_hbm, stat_ref,
    x_ref, s_ref, c_ref, gain_ref, router_ref, fid_ref, bid_ref, out_ref, in_sem, out_sem,
):
    sources = (fid_hbm, bid_hbm, x_hbm, s_hbm, gain_hbm, router_hbm, c_hbm)
    places = (fid_ref, bid_ref, x_ref, s_ref, gain_ref, router_ref, c_ref)
    fetches = [pltpu.make_async_copy(a, b, in_sem.at[n]) for n, (a, b) in enumerate(zip(sources, places))]
    for fetch in fetches:
        fetch.start()
    fetches[0].wait()
    fetches[1].wait()
    choices = [columns(ids) for ids in (fid_ref[0, 0], bid_ref[0, 0], bid_ref[1, 0])]
    table = dispatch_table([choices[0], choices[1], choices[1], choices[2]])
    for fetch in fetches[2:]:
        fetch.wait()
    gain = gain_ref[...].astype(f32)
    rows = []
    for n, wide in enumerate((x_ref[0], s_ref[0, 0], s_ref[1, 0])):
        inverse, normed = norm_rows(wide.astype(f32), gain)
        stat_ref[n] = route(normed, inverse, choices[n], router_ref[...])
        rows.append(normed)
    stacked = jnp.concatenate([rows[0], rows[1], c_ref[0].astype(f32), rows[2]], 0).astype(bf16)
    step = ROWS // EXPERTS
    sends = []
    for e in range(EXPERTS):
        at = pl.ds(e * step, step)
        out_ref[at] = dot(table[e * step : (e + 1) * step].astype(bf16), stacked).astype(bf16)
        sends.append(pltpu.make_async_copy(out_ref.at[at], out_hbm.at[at], out_sem.at[e]))
        sends[-1].start()
    for send in sends:
        send.wait()


def again_kernel(
    sec_ref, y_ref, fnew_ref, b_ref, gnew_ref, gain_ref, router_ref, fid_ref, bid_ref,
    out_ref, x_ref, c_ref, stat_ref, *, last,
):
    first = sec_ref[0, 0] == 0
    final = sec_ref[0, 0] == last
    x = jnp.where(first, fnew_ref[0].astype(f32), y_ref[...].astype(f32))
    c = jnp.where(final, gnew_ref[0].astype(f32), b_ref[...].astype(f32))
    x_ref[...] = x.astype(bf16)
    c_ref[...] = c.astype(bf16)
    choices = [columns(fid_ref[1, 0]), columns(bid_ref[1, 0])]
    inverse, normed = norm_rows(x, gain_ref[...].astype(f32))
    stat_ref[...] = route(normed, inverse, choices[0], router_ref[...])
    half = x.shape[1] // 2
    units = [normed[:, :half], c[:, :half], normed[:, half:], c[:, half:]]
    table = dispatch_table(choices + choices).astype(bf16)
    out_ref[...] = dot(table, jnp.concatenate(units, 0).astype(bf16)).astype(bf16)


def roll_up(value, count):
    return pltpu.roll(value, value.shape[0] - count, 0)


PAIRS = CHIPS // 2
SHARED = PAIRS * BLOCK


def early_half(width):
    offset = iota((PAIRS, BLOCK, width), 1)
    return (offset < 2 * CAP).reshape(SHARED, width), offset.reshape(SHARED, width)


def squeezed(value):
    width = value.shape[1]
    pairs = value.reshape(PAIRS, 2, BLOCK, width)
    one, two = (pairs[:, n].reshape(SHARED, width) for n in range(2))
    return jnp.where(early_half(width)[0], one, pltpu.roll(two, 2 * CAP, 0))


def store_halves(out_ref, columns_, left, right):
    width = left.shape[1]
    early, _ = early_half(width)
    one = jnp.where(early, left, pltpu.roll(right, 2 * CAP, 0))
    two = jnp.where(early, pltpu.roll(left, SHARED - 2 * CAP, 0), right)
    for n, value in enumerate((one, two)):
        out_ref[:, n, :, columns_] = value.reshape(PAIRS, BLOCK, width).astype(bf16)


def experts(pre, grad_act, gu_ref, down_ref, out_ref):
    hidden = grad_act.shape[1]
    early, offset = early_half(hidden)
    forward = jnp.where(early, offset, offset - 2 * CAP) < CAP
    pre_gate, pre_up = pre[:, :hidden], pre[:, hidden:]
    sigma = jax.nn.sigmoid(pre_gate)
    silu = pre_gate * sigma
    active = (silu * pre_up).astype(bf16).astype(f32)
    dg = jnp.sum(jnp.where(forward, 0.0, active * grad_act), 1, keepdims=True)
    grad_up = grad_act * silu
    grad_gate = grad_act * pre_up * sigma * (1.0 + pre_gate * (1.0 - sigma))
    active = jnp.where(forward, active, 0.0).astype(bf16)
    grads = jnp.concatenate([jnp.where(forward, 0.0, grad_gate), jnp.where(forward, 0.0, grad_up)], 1).astype(bf16)
    width = down_ref.shape[1] // 2
    step = 256
    for n in range(0, width, step):
        sides = []
        for at in (n, n + width):
            side = dot(active, down_ref[:, at : at + step])
            sides.append(side + dot(grads, gu_ref[:, at : at + step]))
        store_halves(out_ref, pl.ds(n, step), *sides)
    high = dg.astype(bf16).astype(f32)
    pair = [jnp.broadcast_to(v, (SHARED, PACK)) for v in (high, dg - high)]
    store_halves(out_ref, pl.ds(width, PACK), *pair)


CHUNKS = 4


class Weights:
    def __init__(self, gu_hbm, down_hbm, gu_ref, down_ref, sems):
        self.chunk = gu_hbm.shape[1] // CHUNKS
        at = [pl.ds(n * self.chunk, self.chunk) for n in range(CHUNKS)]
        self.copies = [
            pltpu.make_async_copy(gu_hbm.at[:, a], gu_ref.at[:, a], sems.at[n]) for n, a in enumerate(at)
        ]
        self.copies.append(pltpu.make_async_copy(down_hbm, down_ref, sems.at[CHUNKS]))
        for copy in self.copies:
            copy.start()

    def wait(self, n):
        self.copies[n].wait()


def experts_first_kernel(in_ref, gu_hbm, down_hbm, out_ref, keep_ref, gu_ref, down_ref, sems):
    weights = Weights(gu_hbm, down_hbm, gu_ref, down_ref, sems)
    pre = 0.0
    for n in range(CHUNKS):
        weights.wait(n)
        at = slice(n * weights.chunk, (n + 1) * weights.chunk)
        pre = pre + dot_nt(in_ref[:, at], gu_ref[:, at])
    keep_ref[...] = squeezed(roll_up(pre, 2 * CAP))
    weights.wait(CHUNKS)
    grad_act = squeezed(roll_up(dot_nt(in_ref[...], down_ref[...]), CAP))
    experts(squeezed(pre), grad_act, gu_ref, down_ref, out_ref)


def experts_second_kernel(in_ref, keep_ref, gu_hbm, down_hbm, out_ref, gu_ref, down_ref, sems):
    weights = Weights(gu_hbm, down_hbm, gu_ref, down_ref, sems)
    width = in_ref.shape[1]
    sides = [0.0, 0.0]
    for n in range(CHUNKS):
        weights.wait(n)
        h, at = divmod(n * weights.chunk, width)
        part = dot_nt(in_ref[:, at : at + weights.chunk], gu_ref[:, n * weights.chunk : (n + 1) * weights.chunk])
        sides[h] = sides[h] + part
    pre = squeezed(sides[0] + roll_up(sides[1], 2 * CAP))
    weights.wait(CHUNKS)
    rows = in_ref[...]
    grad_act = dot_nt(rows, down_ref[:, :width]) + roll_up(dot_nt(rows, down_ref[:, width:]), 2 * CAP)
    early, offset = early_half(pre.shape[1])
    forward = jnp.where(early, offset, offset - 2 * CAP) < CAP
    pre = jnp.where(forward, pre, keep_ref[...])
    experts(pre, squeezed(grad_act), gu_ref, down_ref, out_ref)


def combine(in_ref, x, s, cot, x_stat, s_stat, fid, bid, gain, router_rows):
    choices = [columns(fid), columns(bid)]
    col, col_pos, _, _ = tables(choices)
    shape = (TOK, ROWS)
    expert, unit, slot = row_codes(shape, 1)
    blocks = []
    for h in range(2):
        for u in range(2):
            at = slice(u * TOK, (u + 1) * TOK)
            for k in range(2):
                hit = (expert == col[k][at]) & (slot == col_pos[k][at]) & (unit == 2 * h + u)
                blocks.append(jnp.where(hit, 1.0, 0.0))
    table = jnp.concatenate(blocks, 0).astype(bf16)
    picked = dot(table, in_ref[...])
    width = x.shape[1] // 2

    def taken(u, k):
        rows = [picked[((h * 2 + u) * 2 + k) * TOK :][:TOK] for h in range(2)]
        value = jnp.concatenate([r[:, :width] for r in rows], 1)
        return value, rows[0][:, width : width + 1] + rows[1][:, width : width + 1]

    def gates(stat):
        affin = [stat[:, 0:1], stat[:, 1:2]]
        total = affin[0] + affin[1]
        return affin, total, [routed_scale * a / total for a in affin]

    _, _, g = gates(x_stat)
    layer_out = x + (g[0] * taken(0, 0)[0] + g[1] * taken(0, 1)[0])
    affin, total, g = gates(s_stat)
    inverse = s_stat[:, 2:3]
    back0, dg0 = taken(1, 0)
    back1, dg1 = taken(1, 1)
    inner = g[0] * dg0 + g[1] * dg1
    grad_normed = g[0] * back0 + g[1] * back1
    grad_logit = [
        routed_scale / total * (dg - inner / routed_scale) * a * (1.0 - a)
        for dg, a in zip((dg0, dg1), affin)
    ]
    for e in range(EXPERTS):
        share = jnp.where(choices[1][0] == e, grad_logit[0], 0.0)
        share = share + jnp.where(choices[1][1] == e, grad_logit[1], 0.0)
        grad_normed = grad_normed + share * router_rows[e : e + 1].astype(f32)
    scaled = grad_normed * gain
    mean = jnp.mean(scaled * s, -1, keepdims=True)
    grad = cot + inverse * scaled - s * inverse * inverse * inverse * mean
    return layer_out.astype(bf16), grad.astype(bf16)


def combine_first_kernel(
    in_ref, x_ref, s_ref, c_ref, stat_ref, fid_ref, bid_ref, gain_ref, router_ref, y_ref, b_ref
):
    y, b = combine(
        in_ref, x_ref[0].astype(f32), s_ref[0, 0].astype(f32), c_ref[0].astype(f32),
        stat_ref[0], stat_ref[1], fid_ref[0, 0], bid_ref[0, 0],
        gain_ref[...].astype(f32), router_ref[...],
    )
    y_ref[...] = y
    b_ref[...] = b


def combine_second_kernel(
    in_ref, x_ref, s_ref, c_ref, stat_ref, x_stat_ref, fid_ref, bid_ref, gain_ref, router_ref,
    y0_ref, b0_ref, y_ref, b_ref,
):
    y, b = combine(
        in_ref, x_ref[...].astype(f32), s_ref[1, 0].astype(f32), c_ref[...].astype(f32),
        x_stat_ref[...], stat_ref[2], fid_ref[1, 0], bid_ref[1, 0],
        gain_ref[...].astype(f32), router_ref[...],
    )
    y_ref[0, 0] = y0_ref[...]
    b_ref[0, 0] = b0_ref[...]
    y_ref[1, 0] = y
    b_ref[1, 0] = b


VMEM_BYTES = 28 * 2**20
PREPARE_BYTES = 62 * 2**20


def in_hbm(args):
    return [pltpu.with_memory_space_constraint(a, pltpu.HBM) for a in args]


def call(kernel, outs, *args, smem=0, weights=()):
    spec = pl.BlockSpec(memory_space=pltpu.VMEM)
    first = pl.BlockSpec(memory_space=pltpu.SMEM)
    far = pl.BlockSpec(memory_space=pltpu.HBM)
    outs = [jax.ShapeDtypeStruct(*o) for o in outs]
    scratch = []
    if weights:
        scratch = [pltpu.VMEM(w.shape, w.dtype) for w in weights]
        scratch.append(pltpu.SemaphoreType.DMA((CHUNKS + 1,)))
    return pl.pallas_call(
        kernel,
        out_shape=outs,
        in_specs=[first] * smem + [spec] * (len(args) - smem) + [far] * len(weights),
        out_specs=[spec] * len(outs),
        scratch_shapes=scratch,
        compiler_params=pltpu.CompilerParams(vmem_limit_bytes=VMEM_BYTES),
    )(*args, *in_hbm(weights))


def swapped(block):
    return lax.ppermute(block, "core", [(0, 1), (1, 0)])


def exchanged(block):
    block = block.reshape(ROWS, block.shape[-1])
    return lax.all_to_all(block, ("x", "y"), split_axis=0, concat_axis=0, tiled=True)


def shifted(block, distance):
    count = lax.axis_size("pipe")
    route_ = [(i - distance, i) for i in range(count) if 0 <= i - distance < count]
    return lax.ppermute(block, "pipe", route_)


def per_device(
    forward_in, forward_new, grad_in, grad_new, saved_inputs, forward_ids, backward_ids,
    norm_gain, router, gate_proj, up_proj, down_proj,
):
    width = forward_in.shape[-1]
    row = (TOK, width)
    stat = (TOK, 128)
    forward_ids = forward_ids.transpose(0, 1, 3, 2)
    backward_ids = backward_ids.transpose(0, 1, 3, 2)
    router = router[0].T
    args = (forward_in, saved_inputs, grad_in, norm_gain, router, forward_ids, backward_ids)
    sent, stats = pl.pallas_call(
        prepare_kernel,
        out_shape=[jax.ShapeDtypeStruct((ROWS, width), bf16), jax.ShapeDtypeStruct((3, *stat), f32)],
        in_specs=[pl.BlockSpec(memory_space=pltpu.HBM)] * len(args),
        out_specs=[pl.BlockSpec(memory_space=pltpu.HBM), pl.BlockSpec(memory_space=pltpu.VMEM)],
        scratch_shapes=[pltpu.VMEM(a.shape, a.dtype) for a in args]
        + [
            pltpu.VMEM((ROWS, width), bf16),
            pltpu.SemaphoreType.DMA((len(args),)),
            pltpu.SemaphoreType.DMA((EXPERTS,)),
        ],
        compiler_params=pltpu.CompilerParams(vmem_limit_bytes=PREPARE_BYTES),
    )(*in_hbm(args))
    gates_, ups, downs = gate_proj[0], up_proj[0], down_proj[0]
    weights = (
        jnp.concatenate([w.T for w in (gates_, swapped(gates_), ups, swapped(ups))], 0),
        jnp.concatenate([downs, swapped(downs)], 0),
    )
    hidden = weights[0].shape[0]
    packed = (PAIRS, 2, BLOCK, width // 2 + PACK)

    came = exchanged(sent)
    sent, keep = call(
        experts_first_kernel, [(packed, bf16), ((SHARED, hidden), f32)], came, weights=weights
    )
    came = exchanged(sent)
    y0, b0 = call(
        combine_first_kernel, [(row, bf16)] * 2,
        came, forward_in, saved_inputs, grad_in, stats, forward_ids, backward_ids, norm_gain, router,
    )
    section = lax.axis_index("pipe").astype(jnp.int32).reshape(1, 1)
    sent, x1, c1, x1_stat = call(
        functools.partial(again_kernel, last=lax.axis_size("pipe") - 1),
        [((ROWS, width // 2), bf16), (row, bf16), (row, bf16), (stat, f32)],
        section, shifted(y0, 1), forward_new, shifted(b0, -1), grad_new, norm_gain, router,
        forward_ids, backward_ids,
        smem=1,
    )
    came = exchanged(sent)
    (sent,) = call(experts_second_kernel, [(packed, bf16)], came, keep, weights=weights)
    came = exchanged(sent)
    full = (2, 1, *row)
    return tuple(
        call(
            combine_second_kernel, [(full, bf16)] * 2,
            came, x1, saved_inputs, c1, stats, x1_stat, forward_ids, backward_ids, norm_gain, router,
            y0, b0,
        )
    )


def solution(mesh):
    split = Mesh(np.asarray(mesh.devices).reshape(-1, 4, 4, 2), ("pipe", "x", "y", "core"))
    tokens = ("x", "y", "core")
    in_specs = (
        P("pipe", tokens, None),
        P(None, tokens, None),
        P("pipe", tokens, None),
        P(None, tokens, None),
        P(None, "pipe", tokens, None),
        P(None, "pipe", tokens, None),
        P(None, "pipe", tokens, None),
        P("pipe", None),
        P("pipe", None, None),
        P("pipe", None, tokens),
        P("pipe", None, tokens),
        P("pipe", tokens, None),
    )
    out_specs = (P(None, "pipe", tokens, None), P(None, "pipe", tokens, None))
    return jax.shard_map(
        per_device, mesh=split, in_specs=in_specs, out_specs=out_specs, check_vma=False
    )
```

```python
import functools

import jax
import jax.numpy as jnp
import numpy as np
from jax import lax
from jax.experimental import pallas as pl
from jax.experimental.pallas import tpu as pltpu
from jax.sharding import Mesh
from jax.sharding import PartitionSpec as P

CAP = 6
EXPERTS = 4
TOK = 8
CHIPS = 16
UNITS = 4
BLOCK = UNITS * CAP
ROWS = CHIPS * BLOCK
PACK = 128

routed_scale = 2.5
norm_eps = 1e-06
f32 = jnp.float32
bf16 = jnp.bfloat16

NT = (((1,), (1,)), ((), ()))


def dot(a, b):
    return jnp.dot(a, b, preferred_element_type=f32)


def dot_nt(a, b):
    return lax.dot_general(a, b, NT, preferred_element_type=f32)


def iota(shape, axis):
    return lax.broadcasted_iota(jnp.int32, shape, axis)


def whole(index, size):
    return jnp.floor((index.astype(f32) + 0.5) * (1.0 / size))


def row_codes(shape, axis):
    row = iota(shape, axis)
    expert = whole(row, ROWS // EXPERTS)
    offset = row.astype(f32) - BLOCK * whole(row, BLOCK)
    unit = jnp.floor((offset + 0.5) * (1.0 / CAP))
    return expert, unit, offset - CAP * unit


def columns(ids):
    wide = ids.astype(f32)
    here = iota((TOK, TOK), 0) == iota((TOK, TOK), 1)
    return [jnp.sum(jnp.where(here, wide[k : k + 1], 0.0), 1, keepdims=True) for k in range(2)]


def tables(choices):
    col = [jnp.concatenate([c[k] for c in choices], 0) for k in range(2)]
    n = col[0].shape[0]
    i, j = iota((n, n), 0), iota((n, n), 1)
    same = whole(i, TOK) == whole(j, TOK)
    lane = [jnp.sum(jnp.where(i == j, c, 0.0), 0, keepdims=True) for c in col]
    col_pos, lane_pos = [], []
    for k in range(2):
        ahead = same & (j < i) & ((lane[0] == col[k]) | (lane[1] == col[k]))
        col_pos.append(jnp.sum(jnp.where(ahead, 1.0, 0.0), 1, keepdims=True))
        ahead = same & (i < j) & ((col[0] == lane[k]) | (col[1] == lane[k]))
        lane_pos.append(jnp.sum(jnp.where(ahead, 1.0, 0.0), 0, keepdims=True))
    return col, col_pos, lane, lane_pos


def dispatch_table(choices):
    _, _, lane, lane_pos = tables(choices)
    shape = (ROWS, UNITS * TOK)
    expert, unit, slot = row_codes(shape, 0)
    hit = (expert == lane[0]) & (slot == lane_pos[0]) | (expert == lane[1]) & (slot == lane_pos[1])
    hit = hit & (unit == whole(iota(shape, 1), TOK))
    return jnp.where(hit, 1.0, 0.0)


def norm_rows(wide, gain):
    inverse = lax.rsqrt(jnp.mean(wide * wide, -1, keepdims=True) + norm_eps)
    return inverse, (wide * inverse * gain).astype(bf16).astype(f32)


def route(normed, inverse, choice, router):
    logits = dot_nt(normed.astype(bf16), router)
    lanes = iota(logits.shape, 1).astype(f32)
    affin = [
        jax.nn.sigmoid(jnp.sum(jnp.where(lanes == choice[k], logits, 0.0), -1, keepdims=True))
        for k in range(2)
    ]
    at = iota((TOK, 128), 1)
    return jnp.where(at == 0, affin[0], jnp.where(at == 1, affin[1], inverse))


def turned(g_hbm, u_hbm, out_hbm, w_ref, t_ref, sem):
    reads = [pltpu.make_async_copy(w, w_ref.at[n], sem.at[n]) for n, w in enumerate((g_hbm, u_hbm))]
    for read in reads:
        read.start()
    depth, width = w_ref.shape[-2:]
    writes = []
    for n, read in enumerate(reads):
        read.wait()
        rows = pl.ds(n * width, width)
        for at in range(0, depth, 128):
            t_ref[rows, at : at + 128] = w_ref[n, 0, at : at + 128, :].T
        writes.append(pltpu.make_async_copy(t_ref.at[rows], out_hbm.at[rows], sem.at[2 + n]))
        writes[-1].start()
    for write in writes:
        write.wait()


def turn_kernel(core_ref, before_hbm, g_hbm, u_hbm, out_hbm, w_ref, t_ref, sem):
    del before_hbm

    @pl.when(core_ref[0, 0] == 0)
    def _():
        turned(g_hbm, u_hbm, out_hbm, w_ref, t_ref, sem)


def prepare_kernel(
    core_ref, x_hbm, s_hbm, c_hbm, gain_hbm, router_hbm, fid_hbm, bid_hbm, g_hbm, u_hbm,
    out_hbm, stat_ref, turned_hbm,
    x_ref, s_ref, c_ref, gain_ref, router_ref, fid_ref, bid_ref, out_ref, in_sem, out_sem,
    w_ref, t_ref, w_sem,
):
    sources = (fid_hbm, bid_hbm, x_hbm, s_hbm, gain_hbm, router_hbm, c_hbm)
    places = (fid_ref, bid_ref, x_ref, s_ref, gain_ref, router_ref, c_ref)
    fetches = [pltpu.make_async_copy(a, b, in_sem.at[n]) for n, (a, b) in enumerate(zip(sources, places))]
    for fetch in fetches:
        fetch.start()
    fetches[0].wait()
    fetches[1].wait()
    choices = [columns(ids) for ids in (fid_ref[0, 0], bid_ref[0, 0], bid_ref[1, 0])]
    table = dispatch_table([choices[0], choices[1], choices[1], choices[2]])
    for fetch in fetches[2:]:
        fetch.wait()
    gain = gain_ref[...].astype(f32)
    rows = []
    for n, wide in enumerate((x_ref[0], s_ref[0, 0], s_ref[1, 0])):
        inverse, normed = norm_rows(wide.astype(f32), gain)
        stat_ref[n] = route(normed, inverse, choices[n], router_ref[...])
        rows.append(normed)
    stacked = jnp.concatenate([rows[0], rows[1], c_ref[0].astype(f32), rows[2]], 0).astype(bf16)
    step = ROWS // EXPERTS
    sends = []
    for e in range(EXPERTS):
        at = pl.ds(e * step, step)
        out_ref[at] = dot(table[e * step : (e + 1) * step].astype(bf16), stacked).astype(bf16)
        sends.append(pltpu.make_async_copy(out_ref.at[at], out_hbm.at[at], out_sem.at[e]))
        sends[-1].start()

    @pl.when(core_ref[0, 0] == 1)
    def _():
        turned(g_hbm, u_hbm, turned_hbm, w_ref, t_ref, w_sem)

    for send in sends:
        send.wait()


def again_kernel(
    sec_ref, y_ref, fnew_ref, b_ref, gnew_ref, gain_ref, router_ref, fid_ref, bid_ref,
    out_ref, x_ref, c_ref, stat_ref, *, last,
):
    first = sec_ref[0, 0] == 0
    final = sec_ref[0, 0] == last
    x = jnp.where(first, fnew_ref[0].astype(f32), y_ref[...].astype(f32))
    c = jnp.where(final, gnew_ref[0].astype(f32), b_ref[...].astype(f32))
    x_ref[...] = x.astype(bf16)
    c_ref[...] = c.astype(bf16)
    choices = [columns(fid_ref[1, 0]), columns(bid_ref[1, 0])]
    inverse, normed = norm_rows(x, gain_ref[...].astype(f32))
    stat_ref[...] = route(normed, inverse, choices[0], router_ref[...])
    half = x.shape[1] // 2
    units = [normed[:, :half], c[:, :half], normed[:, half:], c[:, half:]]
    table = dispatch_table(choices + choices).astype(bf16)
    out_ref[...] = dot(table, jnp.concatenate(units, 0).astype(bf16)).astype(bf16)


def roll_up(value, count):
    return pltpu.roll(value, value.shape[0] - count, 0)


PAIRS = CHIPS // 2
SHARED = PAIRS * BLOCK


def early_half(width):
    offset = iota((PAIRS, BLOCK, width), 1)
    return (offset < 2 * CAP).reshape(SHARED, width), offset.reshape(SHARED, width)


def squeezed(value):
    width = value.shape[1]
    pairs = value.reshape(PAIRS, 2, BLOCK, width)
    one, two = (pairs[:, n].reshape(SHARED, width) for n in range(2))
    return jnp.where(early_half(width)[0], one, pltpu.roll(two, 2 * CAP, 0))


def store_halves(out_ref, columns_, left, right):
    width = left.shape[1]
    early, _ = early_half(width)
    one = jnp.where(early, left, pltpu.roll(right, 2 * CAP, 0))
    two = jnp.where(early, pltpu.roll(left, SHARED - 2 * CAP, 0), right)
    for n, value in enumerate((one, two)):
        out_ref[:, n, :, columns_] = value.reshape(PAIRS, BLOCK, width).astype(bf16)


def experts(pre, grad_act, gu_ref, down_ref, out_ref):
    hidden = grad_act.shape[1]
    early, offset = early_half(hidden)
    forward = jnp.where(early, offset, offset - 2 * CAP) < CAP
    pre_gate, pre_up = pre[:, :hidden], pre[:, hidden:]
    sigma = jax.nn.sigmoid(pre_gate)
    silu = pre_gate * sigma
    active = (silu * pre_up).astype(bf16).astype(f32)
    dg = jnp.sum(jnp.where(forward, 0.0, active * grad_act), 1, keepdims=True)
    grad_up = grad_act * silu
    grad_gate = grad_act * pre_up * sigma * (1.0 + pre_gate * (1.0 - sigma))
    active = jnp.where(forward, active, 0.0).astype(bf16)
    grads = jnp.concatenate([jnp.where(forward, 0.0, grad_gate), jnp.where(forward, 0.0, grad_up)], 1).astype(bf16)
    width = down_ref.shape[1] // 2
    step = 256
    for n in range(0, width, step):
        sides = []
        for at in (n, n + width):
            side = dot(active, down_ref[:, at : at + step])
            sides.append(side + dot(grads, gu_ref[:, at : at + step]))
        store_halves(out_ref, pl.ds(n, step), *sides)
    high = dg.astype(bf16).astype(f32)
    pair = [jnp.broadcast_to(v, (SHARED, PACK)) for v in (high, dg - high)]
    store_halves(out_ref, pl.ds(width, PACK), *pair)


CHUNKS = 4


class Weights:
    def __init__(self, gu_hbm, down_hbm, gu_ref, down_ref, sems):
        self.chunk = gu_hbm.shape[1] // CHUNKS
        at = [pl.ds(n * self.chunk, self.chunk) for n in range(CHUNKS)]
        self.copies = [
            pltpu.make_async_copy(gu_hbm.at[:, a], gu_ref.at[:, a], sems.at[n]) for n, a in enumerate(at)
        ]
        self.copies.append(pltpu.make_async_copy(down_hbm, down_ref, sems.at[CHUNKS]))
        for copy in self.copies:
            copy.start()

    def wait(self, n):
        self.copies[n].wait()


def experts_first_kernel(in_ref, gu_hbm, down_hbm, out_ref, keep_ref, gu_ref, down_ref, sems):
    weights = Weights(gu_hbm, down_hbm, gu_ref, down_ref, sems)
    pre = 0.0
    for n in range(CHUNKS):
        weights.wait(n)
        at = slice(n * weights.chunk, (n + 1) * weights.chunk)
        pre = pre + dot_nt(in_ref[:, at], gu_ref[:, at])
    keep_ref[...] = squeezed(roll_up(pre, 2 * CAP))
    weights.wait(CHUNKS)
    grad_act = squeezed(roll_up(dot_nt(in_ref[...], down_ref[...]), CAP))
    experts(squeezed(pre), grad_act, gu_ref, down_ref, out_ref)


def experts_second_kernel(in_ref, keep_ref, gu_hbm, down_hbm, out_ref, gu_ref, down_ref, sems):
    weights = Weights(gu_hbm, down_hbm, gu_ref, down_ref, sems)
    width = in_ref.shape[1]
    sides = [0.0, 0.0]
    for n in range(CHUNKS):
        weights.wait(n)
        h, at = divmod(n * weights.chunk, width)
        part = dot_nt(in_ref[:, at : at + weights.chunk], gu_ref[:, n * weights.chunk : (n + 1) * weights.chunk])
        sides[h] = sides[h] + part
    pre = squeezed(sides[0] + roll_up(sides[1], 2 * CAP))
    weights.wait(CHUNKS)
    rows = in_ref[...]
    grad_act = dot_nt(rows, down_ref[:, :width]) + roll_up(dot_nt(rows, down_ref[:, width:]), 2 * CAP)
    early, offset = early_half(pre.shape[1])
    forward = jnp.where(early, offset, offset - 2 * CAP) < CAP
    pre = jnp.where(forward, pre, keep_ref[...])
    experts(pre, squeezed(grad_act), gu_ref, down_ref, out_ref)


def combine(in_ref, x, s, cot, x_stat, s_stat, fid, bid, gain, router_rows):
    choices = [columns(fid), columns(bid)]
    col, col_pos, _, _ = tables(choices)
    shape = (TOK, ROWS)
    expert, unit, slot = row_codes(shape, 1)
    blocks = []
    for h in range(2):
        for u in range(2):
            at = slice(u * TOK, (u + 1) * TOK)
            for k in range(2):
                hit = (expert == col[k][at]) & (slot == col_pos[k][at]) & (unit == 2 * h + u)
                blocks.append(jnp.where(hit, 1.0, 0.0))
    table = jnp.concatenate(blocks, 0).astype(bf16)
    picked = dot(table, in_ref[...])
    width = x.shape[1] // 2

    def taken(u, k):
        rows = [picked[((h * 2 + u) * 2 + k) * TOK :][:TOK] for h in range(2)]
        value = jnp.concatenate([r[:, :width] for r in rows], 1)
        return value, rows[0][:, width : width + 1] + rows[1][:, width : width + 1]

    def gates(stat):
        affin = [stat[:, 0:1], stat[:, 1:2]]
        total = affin[0] + affin[1]
        return affin, total, [routed_scale * a / total for a in affin]

    _, _, g = gates(x_stat)
    layer_out = x + (g[0] * taken(0, 0)[0] + g[1] * taken(0, 1)[0])
    affin, total, g = gates(s_stat)
    inverse = s_stat[:, 2:3]
    back0, dg0 = taken(1, 0)
    back1, dg1 = taken(1, 1)
    inner = g[0] * dg0 + g[1] * dg1
    grad_normed = g[0] * back0 + g[1] * back1
    grad_logit = [
        routed_scale / total * (dg - inner / routed_scale) * a * (1.0 - a)
        for dg, a in zip((dg0, dg1), affin)
    ]
    for e in range(EXPERTS):
        share = jnp.where(choices[1][0] == e, grad_logit[0], 0.0)
        share = share + jnp.where(choices[1][1] == e, grad_logit[1], 0.0)
        grad_normed = grad_normed + share * router_rows[e : e + 1].astype(f32)
    scaled = grad_normed * gain
    mean = jnp.mean(scaled * s, -1, keepdims=True)
    grad = cot + inverse * scaled - s * inverse * inverse * inverse * mean
    return layer_out.astype(bf16), grad.astype(bf16)


def combine_first_kernel(
    in_ref, x_ref, s_ref, c_ref, stat_ref, fid_ref, bid_ref, gain_ref, router_ref, y_ref, b_ref
):
    y, b = combine(
        in_ref, x_ref[0].astype(f32), s_ref[0, 0].astype(f32), c_ref[0].astype(f32),
        stat_ref[0], stat_ref[1], fid_ref[0, 0], bid_ref[0, 0],
        gain_ref[...].astype(f32), router_ref[...],
    )
    y_ref[...] = y
    b_ref[...] = b


def combine_second_kernel(
    in_ref, x_ref, s_ref, c_ref, stat_ref, x_stat_ref, fid_ref, bid_ref, gain_ref, router_ref,
    y0_ref, b0_ref, y_ref, b_ref,
):
    y, b = combine(
        in_ref, x_ref[...].astype(f32), s_ref[1, 0].astype(f32), c_ref[...].astype(f32),
        x_stat_ref[...], stat_ref[2], fid_ref[1, 0], bid_ref[1, 0],
        gain_ref[...].astype(f32), router_ref[...],
    )
    y_ref[0, 0] = y0_ref[...]
    b_ref[0, 0] = b0_ref[...]
    y_ref[1, 0] = y
    b_ref[1, 0] = b


VMEM_BYTES = 28 * 2**20
PREPARE_BYTES = 62 * 2**20


def in_hbm(args):
    return [pltpu.with_memory_space_constraint(a, pltpu.HBM) for a in args]


def call(kernel, outs, *args, smem=0, weights=()):
    spec = pl.BlockSpec(memory_space=pltpu.VMEM)
    first = pl.BlockSpec(memory_space=pltpu.SMEM)
    far = pl.BlockSpec(memory_space=pltpu.HBM)
    outs = [jax.ShapeDtypeStruct(*o) for o in outs]
    scratch = []
    if weights:
        scratch = [pltpu.VMEM(w.shape, w.dtype) for w in weights]
        scratch.append(pltpu.SemaphoreType.DMA((CHUNKS + 1,)))
    return pl.pallas_call(
        kernel,
        out_shape=outs,
        in_specs=[first] * smem + [spec] * (len(args) - smem) + [far] * len(weights),
        out_specs=[spec] * len(outs),
        scratch_shapes=scratch,
        compiler_params=pltpu.CompilerParams(vmem_limit_bytes=VMEM_BYTES),
    )(*args, *in_hbm(weights))


def swapped(block):
    return lax.ppermute(block, "core", [(0, 1), (1, 0)])


def exchanged(block):
    block = block.reshape(ROWS, block.shape[-1])
    return lax.all_to_all(block, ("x", "y"), split_axis=0, concat_axis=0, tiled=True)


def shifted(block, distance):
    count = lax.axis_size("pipe")
    route_ = [(i - distance, i) for i in range(count) if 0 <= i - distance < count]
    return lax.ppermute(block, "pipe", route_)


def per_device(
    forward_in, forward_new, grad_in, grad_new, saved_inputs, forward_ids, backward_ids,
    norm_gain, router, gate_proj, up_proj, down_proj,
):
    width = forward_in.shape[-1]
    row = (TOK, width)
    stat = (TOK, 128)
    forward_ids = forward_ids.transpose(0, 1, 3, 2)
    backward_ids = backward_ids.transpose(0, 1, 3, 2)
    router = router[0].T
    args = (forward_in, saved_inputs, grad_in, norm_gain, router, forward_ids, backward_ids)
    core = lax.axis_index("core").astype(jnp.int32).reshape(1, 1)
    shard = gate_proj.shape[-1]
    turn_scratch = [
        pltpu.VMEM((2, *gate_proj.shape), bf16),
        pltpu.VMEM((2 * shard, width), bf16),
        pltpu.SemaphoreType.DMA((4,)),
    ]
    smem = pl.BlockSpec(memory_space=pltpu.SMEM)
    far = pl.BlockSpec(memory_space=pltpu.HBM)
    rows_of = jax.ShapeDtypeStruct((2 * shard, width), bf16)
    sent, stats, rows_ = pl.pallas_call(
        prepare_kernel,
        out_shape=[
            jax.ShapeDtypeStruct((ROWS, width), bf16), jax.ShapeDtypeStruct((3, *stat), f32), rows_of
        ],
        in_specs=[smem] + [far] * (len(args) + 2),
        out_specs=[far, pl.BlockSpec(memory_space=pltpu.VMEM), far],
        scratch_shapes=[pltpu.VMEM(a.shape, a.dtype) for a in args]
        + [
            pltpu.VMEM((ROWS, width), bf16),
            pltpu.SemaphoreType.DMA((len(args),)),
            pltpu.SemaphoreType.DMA((EXPERTS,)),
        ]
        + turn_scratch,
        compiler_params=pltpu.CompilerParams(vmem_limit_bytes=PREPARE_BYTES),
    )(core, *in_hbm((*args, gate_proj, up_proj)))
    came = exchanged(sent)
    rows_ = pl.pallas_call(
        turn_kernel,
        out_shape=rows_of,
        in_specs=[smem] + [far] * 3,
        out_specs=far,
        scratch_shapes=turn_scratch,
        input_output_aliases={1: 0},
        cost_estimate=pl.CostEstimate(flops=0, bytes_accessed=32 * shard * width, transcendentals=0),
        compiler_params=pltpu.CompilerParams(vmem_limit_bytes=VMEM_BYTES),
    )(core, *in_hbm((rows_, gate_proj, up_proj)))
    gates_, ups, downs = rows_[:shard], rows_[shard:], down_proj[0]
    weights = (
        jnp.concatenate([gates_, swapped(gates_), ups, swapped(ups)], 0),
        jnp.concatenate([downs, swapped(downs)], 0),
    )
    hidden = weights[0].shape[0]
    packed = (PAIRS, 2, BLOCK, width // 2 + PACK)

    sent, keep = call(
        experts_first_kernel, [(packed, bf16), ((SHARED, hidden), f32)], came, weights=weights
    )
    came = exchanged(sent)
    y0, b0 = call(
        combine_first_kernel, [(row, bf16)] * 2,
        came, forward_in, saved_inputs, grad_in, stats, forward_ids, backward_ids, norm_gain, router,
    )
    section = lax.axis_index("pipe").astype(jnp.int32).reshape(1, 1)
    sent, x1, c1, x1_stat = call(
        functools.partial(again_kernel, last=lax.axis_size("pipe") - 1),
        [((ROWS, width // 2), bf16), (row, bf16), (row, bf16), (stat, f32)],
        section, shifted(y0, 1), forward_new, shifted(b0, -1), grad_new, norm_gain, router,
        forward_ids, backward_ids,
        smem=1,
    )
    came = exchanged(sent)
    (sent,) = call(experts_second_kernel, [(packed, bf16)], came, keep, weights=weights)
    came = exchanged(sent)
    full = (2, 1, *row)
    return tuple(
        call(
            combine_second_kernel, [(full, bf16)] * 2,
            came, x1, saved_inputs, c1, stats, x1_stat, forward_ids, backward_ids, norm_gain, router,
            y0, b0,
        )
    )


def solution(mesh):
    split = Mesh(np.asarray(mesh.devices).reshape(-1, 4, 4, 2), ("pipe", "x", "y", "core"))
    tokens = ("x", "y", "core")
    in_specs = (
        P("pipe", tokens, None),
        P(None, tokens, None),
        P("pipe", tokens, None),
        P(None, tokens, None),
        P(None, "pipe", tokens, None),
        P(None, "pipe", tokens, None),
        P(None, "pipe", tokens, None),
        P("pipe", None),
        P("pipe", None, None),
        P("pipe", None, tokens),
        P("pipe", None, tokens),
        P("pipe", tokens, None),
    )
    out_specs = (P(None, "pipe", tokens, None), P(None, "pipe", tokens, None))
    return jax.shard_map(
        per_device, mesh=split, in_specs=in_specs, out_specs=out_specs, check_vma=False
    )
```

```python
import functools

import jax
import jax.numpy as jnp
import numpy as np
from jax import lax
from jax.experimental import pallas as pl
from jax.experimental.pallas import tpu as pltpu
from jax.sharding import Mesh
from jax.sharding import PartitionSpec as P

CAP = 6
EXPERTS = 4
TOK = 8
CHIPS = 16
UNITS = 4
BLOCK = UNITS * CAP
ROWS = CHIPS * BLOCK
PACK = 128

routed_scale = 2.5
norm_eps = 1e-06
f32 = jnp.float32
bf16 = jnp.bfloat16

NT = (((1,), (1,)), ((), ()))


def dot(a, b):
    return jnp.dot(a, b, preferred_element_type=f32)


def dot_nt(a, b):
    return lax.dot_general(a, b, NT, preferred_element_type=f32)


def iota(shape, axis):
    return lax.broadcasted_iota(jnp.int32, shape, axis)


def whole(index, size):
    return jnp.floor((index.astype(f32) + 0.5) * (1.0 / size))


def row_codes(shape, axis):
    row = iota(shape, axis)
    expert = whole(row, ROWS // EXPERTS)
    offset = row.astype(f32) - BLOCK * whole(row, BLOCK)
    unit = jnp.floor((offset + 0.5) * (1.0 / CAP))
    return expert, unit, offset - CAP * unit


def columns(ids):
    wide = ids.astype(f32)
    here = iota((TOK, TOK), 0) == iota((TOK, TOK), 1)
    return [jnp.sum(jnp.where(here, wide[k : k + 1], 0.0), 1, keepdims=True) for k in range(2)]


def tables(choices):
    col = [jnp.concatenate([c[k] for c in choices], 0) for k in range(2)]
    n = col[0].shape[0]
    i, j = iota((n, n), 0), iota((n, n), 1)
    same = whole(i, TOK) == whole(j, TOK)
    lane = [jnp.sum(jnp.where(i == j, c, 0.0), 0, keepdims=True) for c in col]
    col_pos, lane_pos = [], []
    for k in range(2):
        ahead = same & (j < i) & ((lane[0] == col[k]) | (lane[1] == col[k]))
        col_pos.append(jnp.sum(jnp.where(ahead, 1.0, 0.0), 1, keepdims=True))
        ahead = same & (i < j) & ((col[0] == lane[k]) | (col[1] == lane[k]))
        lane_pos.append(jnp.sum(jnp.where(ahead, 1.0, 0.0), 0, keepdims=True))
    return col, col_pos, lane, lane_pos


def dispatch_table(choices):
    _, _, lane, lane_pos = tables(choices)
    shape = (ROWS, UNITS * TOK)
    expert, unit, slot = row_codes(shape, 0)
    hit = (expert == lane[0]) & (slot == lane_pos[0]) | (expert == lane[1]) & (slot == lane_pos[1])
    hit = hit & (unit == whole(iota(shape, 1), TOK))
    return jnp.where(hit, 1.0, 0.0)


def norm_rows(wide, gain):
    inverse = lax.rsqrt(jnp.mean(wide * wide, -1, keepdims=True) + norm_eps)
    return inverse, (wide * inverse * gain).astype(bf16).astype(f32)


def route(normed, inverse, choice, router):
    logits = dot_nt(normed.astype(bf16), router)
    lanes = iota(logits.shape, 1).astype(f32)
    affin = [
        jax.nn.sigmoid(jnp.sum(jnp.where(lanes == choice[k], logits, 0.0), -1, keepdims=True))
        for k in range(2)
    ]
    at = iota((TOK, 128), 1)
    return jnp.where(at == 0, affin[0], jnp.where(at == 1, affin[1], inverse))


def prepare_kernel(
    x_hbm, s_hbm, c_hbm, gain_hbm, router_hbm, fid_hbm, bid_hbm, out_hbm, stat_ref,
    x_ref, s_ref, c_ref, gain_ref, router_ref, fid_ref, bid_ref, out_ref, in_sem, out_sem,
):
    sources = (fid_hbm, bid_hbm, x_hbm, s_hbm, gain_hbm, router_hbm, c_hbm)
    places = (fid_ref, bid_ref, x_ref, s_ref, gain_ref, router_ref, c_ref)
    fetches = [pltpu.make_async_copy(a, b, in_sem.at[n]) for n, (a, b) in enumerate(zip(sources, places))]
    for fetch in fetches:
        fetch.start()
    fetches[0].wait()
    fetches[1].wait()
    choices = [columns(ids) for ids in (fid_ref[0, 0], bid_ref[0, 0], bid_ref[1, 0])]
    table = dispatch_table([choices[0], choices[1], choices[1], choices[2]])
    for fetch in fetches[2:]:
        fetch.wait()
    gain = gain_ref[...].astype(f32)
    rows = []
    for n, wide in enumerate((x_ref[0], s_ref[0, 0], s_ref[1, 0])):
        inverse, normed = norm_rows(wide.astype(f32), gain)
        stat_ref[n] = route(normed, inverse, choices[n], router_ref[...])
        rows.append(normed)
    stacked = jnp.concatenate([rows[0], rows[1], c_ref[0].astype(f32), rows[2]], 0).astype(bf16)
    step = ROWS // EXPERTS
    part = step // 2
    sends = []
    for e in range(EXPERTS):
        at = pl.ds(e * part, part)
        out_ref[at] = dot(table[e * step : e * step + part].astype(bf16), stacked).astype(bf16)
        for n in range(2):
            place = out_hbm.at[pl.ds(e * step + n * part, part)]
            sends.append(pltpu.make_async_copy(out_ref.at[at], place, out_sem.at[2 * e + n]))
            sends[-1].start()
    for send in sends:
        send.wait()


def again_kernel(
    sec_ref, y_ref, fnew_ref, b_ref, gnew_ref, gain_ref, router_ref, fid_ref, bid_ref,
    out_ref, x_ref, c_ref, stat_ref, *, last,
):
    first = sec_ref[0, 0] == 0
    final = sec_ref[0, 0] == last
    x = jnp.where(first, fnew_ref[0].astype(f32), y_ref[...].astype(f32))
    c = jnp.where(final, gnew_ref[0].astype(f32), b_ref[...].astype(f32))
    x_ref[...] = x.astype(bf16)
    c_ref[...] = c.astype(bf16)
    choices = [columns(fid_ref[1, 0]), columns(bid_ref[1, 0])]
    inverse, normed = norm_rows(x, gain_ref[...].astype(f32))
    stat_ref[...] = route(normed, inverse, choices[0], router_ref[...])
    half = x.shape[1] // 2
    units = [normed[:, :half], c[:, :half], normed[:, half:], c[:, half:]]
    table = dispatch_table(choices + choices).astype(bf16)
    out_ref[...] = dot(table, jnp.concatenate(units, 0).astype(bf16)).astype(bf16)


def roll_up(value, count):
    return pltpu.roll(value, value.shape[0] - count, 0)


PAIRS = CHIPS // 2
SHARED = PAIRS * BLOCK


def early_half(width):
    offset = iota((PAIRS, BLOCK, width), 1)
    return (offset < 2 * CAP).reshape(SHARED, width), offset.reshape(SHARED, width)


def squeezed(value):
    width = value.shape[1]
    pairs = value.reshape(PAIRS, 2, BLOCK, width)
    one, two = (pairs[:, n].reshape(SHARED, width) for n in range(2))
    return jnp.where(early_half(width)[0], one, pltpu.roll(two, 2 * CAP, 0))


def store_halves(out_ref, columns_, left, right):
    width = left.shape[1]
    early, _ = early_half(width)
    one = jnp.where(early, left, pltpu.roll(right, 2 * CAP, 0))
    two = jnp.where(early, pltpu.roll(left, SHARED - 2 * CAP, 0), right)
    for n, value in enumerate((one, two)):
        out_ref[:, n, :, columns_] = value.reshape(PAIRS, BLOCK, width).astype(bf16)


def experts(pre, grad_act, gu_ref, down_ref, out_ref):
    hidden = grad_act.shape[1]
    early, offset = early_half(hidden)
    forward = jnp.where(early, offset, offset - 2 * CAP) < CAP
    pre_gate, pre_up = pre[:, :hidden], pre[:, hidden:]
    sigma = jax.nn.sigmoid(pre_gate)
    silu = pre_gate * sigma
    active = (silu * pre_up).astype(bf16).astype(f32)
    dg = jnp.sum(jnp.where(forward, 0.0, active * grad_act), 1, keepdims=True)
    grad_up = grad_act * silu
    grad_gate = grad_act * pre_up * sigma * (1.0 + pre_gate * (1.0 - sigma))
    active = jnp.where(forward, active, 0.0).astype(bf16)
    grads = jnp.concatenate([jnp.where(forward, 0.0, grad_gate), jnp.where(forward, 0.0, grad_up)], 1).astype(bf16)
    width = down_ref.shape[1] // 2
    step = 256
    for n in range(0, width, step):
        sides = []
        for at in (n, n + width):
            side = dot(active, down_ref[:, at : at + step])
            sides.append(side + dot(grads, gu_ref[:, at : at + step]))
        store_halves(out_ref, pl.ds(n, step), *sides)
    high = dg.astype(bf16).astype(f32)
    pair = [jnp.broadcast_to(v, (SHARED, PACK)) for v in (high, dg - high)]
    store_halves(out_ref, pl.ds(width, PACK), *pair)


CHUNKS = 4


class Weights:
    def __init__(self, gu_hbm, down_hbm, gu_ref, down_ref, sems):
        self.chunk = gu_hbm.shape[1] // CHUNKS
        at = [pl.ds(n * self.chunk, self.chunk) for n in range(CHUNKS)]
        self.copies = [
            pltpu.make_async_copy(gu_hbm.at[:, a], gu_ref.at[:, a], sems.at[n]) for n, a in enumerate(at)
        ]
        self.copies.append(pltpu.make_async_copy(down_hbm, down_ref, sems.at[CHUNKS]))
        for copy in self.copies:
            copy.start()

    def wait(self, n):
        self.copies[n].wait()


def experts_first_kernel(in_ref, gu_hbm, down_hbm, out_ref, keep_ref, gu_ref, down_ref, sems):
    weights = Weights(gu_hbm, down_hbm, gu_ref, down_ref, sems)
    pre = 0.0
    for n in range(CHUNKS):
        weights.wait(n)
        at = slice(n * weights.chunk, (n + 1) * weights.chunk)
        pre = pre + dot_nt(in_ref[:, at], gu_ref[:, at])
    keep_ref[...] = squeezed(roll_up(pre, 2 * CAP))
    weights.wait(CHUNKS)
    grad_act = squeezed(roll_up(dot_nt(in_ref[...], down_ref[...]), CAP))
    experts(squeezed(pre), grad_act, gu_ref, down_ref, out_ref)


def experts_second_kernel(in_ref, keep_ref, gu_hbm, down_hbm, out_ref, gu_ref, down_ref, sems):
    weights = Weights(gu_hbm, down_hbm, gu_ref, down_ref, sems)
    width = in_ref.shape[1]
    sides = [0.0, 0.0]
    for n in range(CHUNKS):
        weights.wait(n)
        h, at = divmod(n * weights.chunk, width)
        part = dot_nt(in_ref[:, at : at + weights.chunk], gu_ref[:, n * weights.chunk : (n + 1) * weights.chunk])
        sides[h] = sides[h] + part
    pre = squeezed(sides[0] + roll_up(sides[1], 2 * CAP))
    weights.wait(CHUNKS)
    rows = in_ref[...]
    grad_act = dot_nt(rows, down_ref[:, :width]) + roll_up(dot_nt(rows, down_ref[:, width:]), 2 * CAP)
    early, offset = early_half(pre.shape[1])
    forward = jnp.where(early, offset, offset - 2 * CAP) < CAP
    pre = jnp.where(forward, pre, keep_ref[...])
    experts(pre, squeezed(grad_act), gu_ref, down_ref, out_ref)


def combine(in_ref, x, s, cot, x_stat, s_stat, fid, bid, gain, router_rows):
    choices = [columns(fid), columns(bid)]
    col, col_pos, _, _ = tables(choices)
    shape = (TOK, ROWS)
    expert, unit, slot = row_codes(shape, 1)
    blocks = []
    for h in range(2):
        for u in range(2):
            at = slice(u * TOK, (u + 1) * TOK)
            for k in range(2):
                hit = (expert == col[k][at]) & (slot == col_pos[k][at]) & (unit == 2 * h + u)
                blocks.append(jnp.where(hit, 1.0, 0.0))
    table = jnp.concatenate(blocks, 0).astype(bf16)
    picked = dot(table, in_ref[...])
    width = x.shape[1] // 2

    def taken(u, k):
        rows = [picked[((h * 2 + u) * 2 + k) * TOK :][:TOK] for h in range(2)]
        value = jnp.concatenate([r[:, :width] for r in rows], 1)
        return value, rows[0][:, width : width + 1] + rows[1][:, width : width + 1]

    def gates(stat):
        affin = [stat[:, 0:1], stat[:, 1:2]]
        total = affin[0] + affin[1]
        return affin, total, [routed_scale * a / total for a in affin]

    _, _, g = gates(x_stat)
    layer_out = x + (g[0] * taken(0, 0)[0] + g[1] * taken(0, 1)[0])
    affin, total, g = gates(s_stat)
    inverse = s_stat[:, 2:3]
    back0, dg0 = taken(1, 0)
    back1, dg1 = taken(1, 1)
    inner = g[0] * dg0 + g[1] * dg1
    grad_normed = g[0] * back0 + g[1] * back1
    grad_logit = [
        routed_scale / total * (dg - inner / routed_scale) * a * (1.0 - a)
        for dg, a in zip((dg0, dg1), affin)
    ]
    for e in range(EXPERTS):
        share = jnp.where(choices[1][0] == e, grad_logit[0], 0.0)
        share = share + jnp.where(choices[1][1] == e, grad_logit[1], 0.0)
        grad_normed = grad_normed + share * router_rows[e : e + 1].astype(f32)
    scaled = grad_normed * gain
    mean = jnp.mean(scaled * s, -1, keepdims=True)
    grad = cot + inverse * scaled - s * inverse * inverse * inverse * mean
    return layer_out.astype(bf16), grad.astype(bf16)


def combine_first_kernel(
    in_ref, x_ref, s_ref, c_ref, stat_ref, fid_ref, bid_ref, gain_ref, router_ref, y_ref, b_ref
):
    y, b = combine(
        in_ref, x_ref[0].astype(f32), s_ref[0, 0].astype(f32), c_ref[0].astype(f32),
        stat_ref[0], stat_ref[1], fid_ref[0, 0], bid_ref[0, 0],
        gain_ref[...].astype(f32), router_ref[...],
    )
    y_ref[...] = y
    b_ref[...] = b


def combine_second_kernel(
    in_ref, x_ref, s_ref, c_ref, stat_ref, x_stat_ref, fid_ref, bid_ref, gain_ref, router_ref,
    y0_ref, b0_ref, y_ref, b_ref,
):
    y, b = combine(
        in_ref, x_ref[...].astype(f32), s_ref[1, 0].astype(f32), c_ref[...].astype(f32),
        x_stat_ref[...], stat_ref[2], fid_ref[1, 0], bid_ref[1, 0],
        gain_ref[...].astype(f32), router_ref[...],
    )
    y_ref[0, 0] = y0_ref[...]
    b_ref[0, 0] = b0_ref[...]
    y_ref[1, 0] = y
    b_ref[1, 0] = b


VMEM_BYTES = 28 * 2**20
PREPARE_BYTES = 62 * 2**20


def in_hbm(args):
    return [pltpu.with_memory_space_constraint(a, pltpu.HBM) for a in args]


def call(kernel, outs, *args, smem=0, weights=()):
    spec = pl.BlockSpec(memory_space=pltpu.VMEM)
    first = pl.BlockSpec(memory_space=pltpu.SMEM)
    far = pl.BlockSpec(memory_space=pltpu.HBM)
    outs = [jax.ShapeDtypeStruct(*o) for o in outs]
    scratch = []
    if weights:
        scratch = [pltpu.VMEM(w.shape, w.dtype) for w in weights]
        scratch.append(pltpu.SemaphoreType.DMA((CHUNKS + 1,)))
    return pl.pallas_call(
        kernel,
        out_shape=outs,
        in_specs=[first] * smem + [spec] * (len(args) - smem) + [far] * len(weights),
        out_specs=[spec] * len(outs),
        scratch_shapes=scratch,
        compiler_params=pltpu.CompilerParams(vmem_limit_bytes=VMEM_BYTES),
    )(*args, *in_hbm(weights))


def swapped(block):
    return lax.ppermute(block, "core", [(0, 1), (1, 0)])


def exchanged(block):
    block = block.reshape(ROWS, block.shape[-1])
    return lax.all_to_all(block, ("x", "y"), split_axis=0, concat_axis=0, tiled=True)


def shifted(block, distance):
    count = lax.axis_size("pipe")
    route_ = [(i - distance, i) for i in range(count) if 0 <= i - distance < count]
    return lax.ppermute(block, "pipe", route_)


def per_device(
    forward_in, forward_new, grad_in, grad_new, saved_inputs, forward_ids, backward_ids,
    norm_gain, router, gate_proj, up_proj, down_proj,
):
    width = forward_in.shape[-1]
    row = (TOK, width)
    stat = (TOK, 128)
    forward_ids = forward_ids.transpose(0, 1, 3, 2)
    backward_ids = backward_ids.transpose(0, 1, 3, 2)
    router = router[0].T
    args = (forward_in, saved_inputs, grad_in, norm_gain, router, forward_ids, backward_ids)
    sent, stats = pl.pallas_call(
        prepare_kernel,
        out_shape=[jax.ShapeDtypeStruct((ROWS, width), bf16), jax.ShapeDtypeStruct((3, *stat), f32)],
        in_specs=[pl.BlockSpec(memory_space=pltpu.HBM)] * len(args),
        out_specs=[pl.BlockSpec(memory_space=pltpu.HBM), pl.BlockSpec(memory_space=pltpu.VMEM)],
        scratch_shapes=[pltpu.VMEM(a.shape, a.dtype) for a in args]
        + [
            pltpu.VMEM((ROWS // 2, width), bf16),
            pltpu.SemaphoreType.DMA((len(args),)),
            pltpu.SemaphoreType.DMA((2 * EXPERTS,)),
        ],
        compiler_params=pltpu.CompilerParams(vmem_limit_bytes=PREPARE_BYTES),
    )(*in_hbm(args))
    gates_, ups, downs = gate_proj[0], up_proj[0], down_proj[0]
    weights = (
        jnp.concatenate([w.T for w in (gates_, swapped(gates_), ups, swapped(ups))], 0),
        jnp.concatenate([downs, swapped(downs)], 0),
    )
    hidden = weights[0].shape[0]
    packed = (PAIRS, 2, BLOCK, width // 2 + PACK)

    came = exchanged(sent)
    sent, keep = call(
        experts_first_kernel, [(packed, bf16), ((SHARED, hidden), f32)], came, weights=weights
    )
    came = exchanged(sent)
    y0, b0 = call(
        combine_first_kernel, [(row, bf16)] * 2,
        came, forward_in, saved_inputs, grad_in, stats, forward_ids, backward_ids, norm_gain, router,
    )
    section = lax.axis_index("pipe").astype(jnp.int32).reshape(1, 1)
    sent, x1, c1, x1_stat = call(
        functools.partial(again_kernel, last=lax.axis_size("pipe") - 1),
        [((ROWS, width // 2), bf16), (row, bf16), (row, bf16), (stat, f32)],
        section, shifted(y0, 1), forward_new, shifted(b0, -1), grad_new, norm_gain, router,
        forward_ids, backward_ids,
        smem=1,
    )
    came = exchanged(sent)
    (sent,) = call(experts_second_kernel, [(packed, bf16)], came, keep, weights=weights)
    came = exchanged(sent)
    full = (2, 1, *row)
    return tuple(
        call(
            combine_second_kernel, [(full, bf16)] * 2,
            came, x1, saved_inputs, c1, stats, x1_stat, forward_ids, backward_ids, norm_gain, router,
            y0, b0,
        )
    )


def solution(mesh):
    split = Mesh(np.asarray(mesh.devices).reshape(-1, 4, 4, 2), ("pipe", "x", "y", "core"))
    tokens = ("x", "y", "core")
    in_specs = (
        P("pipe", tokens, None),
        P(None, tokens, None),
        P("pipe", tokens, None),
        P(None, tokens, None),
        P(None, "pipe", tokens, None),
        P(None, "pipe", tokens, None),
        P(None, "pipe", tokens, None),
        P("pipe", None),
        P("pipe", None, None),
        P("pipe", None, tokens),
        P("pipe", None, tokens),
        P("pipe", tokens, None),
    )
    out_specs = (P(None, "pipe", tokens, None), P(None, "pipe", tokens, None))
    return jax.shard_map(
        per_device, mesh=split, in_specs=in_specs, out_specs=out_specs, check_vma=False
    )
```

```python
import functools

import jax
import jax.numpy as jnp
import numpy as np
from jax import lax
from jax.experimental import pallas as pl
from jax.experimental.pallas import tpu as pltpu
from jax.sharding import Mesh
from jax.sharding import PartitionSpec as P

CAP = 6
EXPERTS = 4
TOK = 8
CHIPS = 16
UNITS = 4
BLOCK = UNITS * CAP
ROWS = CHIPS * BLOCK
PACK = 128

routed_scale = 2.5
norm_eps = 1e-06
f32 = jnp.float32
bf16 = jnp.bfloat16

NT = (((1,), (1,)), ((), ()))


def dot(a, b):
    return jnp.dot(a, b, preferred_element_type=f32)


def dot_nt(a, b):
    return lax.dot_general(a, b, NT, preferred_element_type=f32)


def iota(shape, axis):
    return lax.broadcasted_iota(jnp.int32, shape, axis)


def whole(index, size):
    return jnp.floor((index.astype(f32) + 0.5) * (1.0 / size))


def row_codes(shape, axis):
    row = iota(shape, axis)
    expert = whole(row, ROWS // EXPERTS)
    offset = row.astype(f32) - BLOCK * whole(row, BLOCK)
    unit = jnp.floor((offset + 0.5) * (1.0 / CAP))
    return expert, unit, offset - CAP * unit


def columns(ids):
    wide = ids.astype(f32)
    here = iota((TOK, TOK), 0) == iota((TOK, TOK), 1)
    return [jnp.sum(jnp.where(here, wide[k : k + 1], 0.0), 1, keepdims=True) for k in range(2)]


def tables(choices):
    col = [jnp.concatenate([c[k] for c in choices], 0) for k in range(2)]
    n = col[0].shape[0]
    i, j = iota((n, n), 0), iota((n, n), 1)
    same = whole(i, TOK) == whole(j, TOK)
    lane = [jnp.sum(jnp.where(i == j, c, 0.0), 0, keepdims=True) for c in col]
    col_pos, lane_pos = [], []
    for k in range(2):
        ahead = same & (j < i) & ((lane[0] == col[k]) | (lane[1] == col[k]))
        col_pos.append(jnp.sum(jnp.where(ahead, 1.0, 0.0), 1, keepdims=True))
        ahead = same & (i < j) & ((col[0] == lane[k]) | (col[1] == lane[k]))
        lane_pos.append(jnp.sum(jnp.where(ahead, 1.0, 0.0), 0, keepdims=True))
    return col, col_pos, lane, lane_pos


def dispatch_table(choices):
    _, _, lane, lane_pos = tables(choices)
    shape = (ROWS, UNITS * TOK)
    expert, unit, slot = row_codes(shape, 0)
    hit = (expert == lane[0]) & (slot == lane_pos[0]) | (expert == lane[1]) & (slot == lane_pos[1])
    hit = hit & (unit == whole(iota(shape, 1), TOK))
    return jnp.where(hit, 1.0, 0.0)


def norm_rows(wide, gain):
    inverse = lax.rsqrt(jnp.mean(wide * wide, -1, keepdims=True) + norm_eps)
    return inverse, (wide * inverse * gain).astype(bf16).astype(f32)


def route(normed, inverse, choice, router):
    logits = dot_nt(normed.astype(bf16), router)
    lanes = iota(logits.shape, 1).astype(f32)
    affin = [
        jax.nn.sigmoid(jnp.sum(jnp.where(lanes == choice[k], logits, 0.0), -1, keepdims=True))
        for k in range(2)
    ]
    at = iota((TOK, 128), 1)
    return jnp.where(at == 0, affin[0], jnp.where(at == 1, affin[1], inverse))


def prepare_kernel(
    x_hbm, s_hbm, c_hbm, gain_hbm, router_hbm, fid_hbm, bid_hbm, out_hbm, stat_ref,
    x_ref, s_ref, c_ref, gain_ref, router_ref, fid_ref, bid_ref, out_ref, in_sem, out_sem,
):
    sources = (fid_hbm, bid_hbm, x_hbm, s_hbm, gain_hbm, router_hbm, c_hbm)
    places = (fid_ref, bid_ref, x_ref, s_ref, gain_ref, router_ref, c_ref)
    fetches = [pltpu.make_async_copy(a, b, in_sem.at[n]) for n, (a, b) in enumerate(zip(sources, places))]
    for fetch in fetches:
        fetch.start()
    fetches[0].wait()
    fetches[1].wait()
    choices = [columns(ids) for ids in (fid_ref[0, 0], bid_ref[0, 0], bid_ref[1, 0])]
    table = dispatch_table([choices[0], choices[1], choices[1], choices[2]])
    for fetch in fetches[2:]:
        fetch.wait()
    gain = gain_ref[...].astype(f32)
    rows = []
    for n, wide in enumerate((x_ref[0], s_ref[0, 0], s_ref[1, 0])):
        inverse, normed = norm_rows(wide.astype(f32), gain)
        stat_ref[n] = route(normed, inverse, choices[n], router_ref[...])
        rows.append(normed)
    stacked = jnp.concatenate([rows[0], rows[1], c_ref[0].astype(f32), rows[2]], 0).astype(bf16)
    step = ROWS // EXPERTS
    part = step // 2
    sends = []
    for e in range(EXPERTS):
        at = pl.ds(e * part, part)
        out_ref[at] = dot(table[e * step : e * step + part].astype(bf16), stacked).astype(bf16)
        for n in range(2):
            place = out_hbm.at[pl.ds(e * step + n * part, part)]
            sends.append(pltpu.make_async_copy(out_ref.at[at], place, out_sem.at[2 * e + n]))
            sends[-1].start()
    for send in sends:
        send.wait()


def again_kernel(
    sec_ref, y_ref, fnew_ref, b_ref, gnew_ref, gain_ref, router_ref, fid_ref, bid_ref,
    out_ref, x_ref, c_ref, stat_ref, *, last,
):
    first = sec_ref[0, 0] == 0
    final = sec_ref[0, 0] == last
    x = jnp.where(first, fnew_ref[0].astype(f32), y_ref[...].astype(f32))
    c = jnp.where(final, gnew_ref[0].astype(f32), b_ref[...].astype(f32))
    x_ref[...] = x.astype(bf16)
    c_ref[...] = c.astype(bf16)
    choices = [columns(fid_ref[1, 0]), columns(bid_ref[1, 0])]
    inverse, normed = norm_rows(x, gain_ref[...].astype(f32))
    stat_ref[...] = route(normed, inverse, choices[0], router_ref[...])
    half = x.shape[1] // 2
    units = [normed[:, :half], c[:, :half], normed[:, half:], c[:, half:]]
    table = dispatch_table(choices + choices).astype(bf16)
    out_ref[...] = dot(table, jnp.concatenate(units, 0).astype(bf16)).astype(bf16)


def roll_up(value, count):
    return pltpu.roll(value, value.shape[0] - count, 0)


PAIRS = CHIPS // 2
SHARED = PAIRS * BLOCK


def early_half(width):
    offset = iota((PAIRS, BLOCK, width), 1)
    return (offset < 2 * CAP).reshape(SHARED, width), offset.reshape(SHARED, width)


def squeezed(value):
    width = value.shape[1]
    pairs = value.reshape(PAIRS, 2, BLOCK, width)
    one, two = (pairs[:, n].reshape(SHARED, width) for n in range(2))
    return jnp.where(early_half(width)[0], one, pltpu.roll(two, 2 * CAP, 0))


def store_halves(out_ref, columns_, left, right):
    width = left.shape[1]
    early, _ = early_half(width)
    one = jnp.where(early, left, pltpu.roll(right, 2 * CAP, 0))
    two = jnp.where(early, pltpu.roll(left, SHARED - 2 * CAP, 0), right)
    for n, value in enumerate((one, two)):
        out_ref[:, n, :, columns_] = value.reshape(PAIRS, BLOCK, width).astype(bf16)


def experts(pre, grad_act, gu_ref, down_ref, out_ref):
    hidden = grad_act.shape[1]
    early, offset = early_half(hidden)
    forward = jnp.where(early, offset, offset - 2 * CAP) < CAP
    pre_gate, pre_up = pre[:, :hidden], pre[:, hidden:]
    sigma = jax.nn.sigmoid(pre_gate)
    silu = pre_gate * sigma
    active = (silu * pre_up).astype(bf16).astype(f32)
    dg = jnp.sum(jnp.where(forward, 0.0, active * grad_act), 1, keepdims=True)
    grad_up = grad_act * silu
    grad_gate = grad_act * pre_up * sigma * (1.0 + pre_gate * (1.0 - sigma))
    active = jnp.where(forward, active, 0.0).astype(bf16)
    grads = jnp.concatenate([jnp.where(forward, 0.0, grad_gate), jnp.where(forward, 0.0, grad_up)], 1).astype(bf16)
    width = down_ref.shape[1] // 2
    step = 256
    for n in range(0, width, step):
        sides = []
        for at in (n, n + width):
            side = dot(active, down_ref[:, at : at + step])
            sides.append(side + dot(grads, gu_ref[:, at : at + step]))
        store_halves(out_ref, pl.ds(n, step), *sides)
    high = dg.astype(bf16).astype(f32)
    pair = [jnp.broadcast_to(v, (SHARED, PACK)) for v in (high, dg - high)]
    store_halves(out_ref, pl.ds(width, PACK), *pair)


CHUNKS = 4


class Weights:
    def __init__(self, gu_hbm, down_hbm, gu_ref, down_ref, sems):
        self.chunk = gu_hbm.shape[1] // CHUNKS
        at = [pl.ds(n * self.chunk, self.chunk) for n in range(CHUNKS)]
        self.copies = [
            pltpu.make_async_copy(gu_hbm.at[:, a], gu_ref.at[:, a], sems.at[n]) for n, a in enumerate(at)
        ]
        self.copies.append(pltpu.make_async_copy(down_hbm, down_ref, sems.at[CHUNKS]))
        for copy in self.copies[-1:] + self.copies[:-1]:
            copy.start()

    def wait(self, n):
        self.copies[n].wait()


def experts_first_kernel(in_ref, gu_hbm, down_hbm, out_ref, keep_ref, gu_ref, down_ref, sems):
    weights = Weights(gu_hbm, down_hbm, gu_ref, down_ref, sems)
    weights.wait(CHUNKS)
    grad_act = squeezed(roll_up(dot_nt(in_ref[...], down_ref[...]), CAP))
    pre = 0.0
    for n in range(CHUNKS):
        weights.wait(n)
        at = slice(n * weights.chunk, (n + 1) * weights.chunk)
        pre = pre + dot_nt(in_ref[:, at], gu_ref[:, at])
    keep_ref[...] = squeezed(roll_up(pre, 2 * CAP))
    experts(squeezed(pre), grad_act, gu_ref, down_ref, out_ref)


def experts_second_kernel(in_ref, keep_ref, gu_hbm, down_hbm, out_ref, gu_ref, down_ref, sems):
    weights = Weights(gu_hbm, down_hbm, gu_ref, down_ref, sems)
    width = in_ref.shape[1]
    weights.wait(CHUNKS)
    rows = in_ref[...]
    grad_act = dot_nt(rows, down_ref[:, :width]) + roll_up(dot_nt(rows, down_ref[:, width:]), 2 * CAP)
    sides = [0.0, 0.0]
    for n in range(CHUNKS):
        weights.wait(n)
        h, at = divmod(n * weights.chunk, width)
        part = dot_nt(in_ref[:, at : at + weights.chunk], gu_ref[:, n * weights.chunk : (n + 1) * weights.chunk])
        sides[h] = sides[h] + part
    pre = squeezed(sides[0] + roll_up(sides[1], 2 * CAP))
    early, offset = early_half(pre.shape[1])
    forward = jnp.where(early, offset, offset - 2 * CAP) < CAP
    pre = jnp.where(forward, pre, keep_ref[...])
    experts(pre, squeezed(grad_act), gu_ref, down_ref, out_ref)


def combine(in_ref, x, s, cot, x_stat, s_stat, fid, bid, gain, router_rows):
    choices = [columns(fid), columns(bid)]
    col, col_pos, _, _ = tables(choices)
    shape = (TOK, ROWS)
    expert, unit, slot = row_codes(shape, 1)
    blocks = []
    for h in range(2):
        for u in range(2):
            at = slice(u * TOK, (u + 1) * TOK)
            for k in range(2):
                hit = (expert == col[k][at]) & (slot == col_pos[k][at]) & (unit == 2 * h + u)
                blocks.append(jnp.where(hit, 1.0, 0.0))
    table = jnp.concatenate(blocks, 0).astype(bf16)
    picked = dot(table, in_ref[...])
    width = x.shape[1] // 2

    def taken(u, k):
        rows = [picked[((h * 2 + u) * 2 + k) * TOK :][:TOK] for h in range(2)]
        value = jnp.concatenate([r[:, :width] for r in rows], 1)
        return value, rows[0][:, width : width + 1] + rows[1][:, width : width + 1]

    def gates(stat):
        affin = [stat[:, 0:1], stat[:, 1:2]]
        total = affin[0] + affin[1]
        return affin, total, [routed_scale * a / total for a in affin]

    _, _, g = gates(x_stat)
    layer_out = x + (g[0] * taken(0, 0)[0] + g[1] * taken(0, 1)[0])
    affin, total, g = gates(s_stat)
    inverse = s_stat[:, 2:3]
    back0, dg0 = taken(1, 0)
    back1, dg1 = taken(1, 1)
    inner = g[0] * dg0 + g[1] * dg1
    grad_normed = g[0] * back0 + g[1] * back1
    grad_logit = [
        routed_scale / total * (dg - inner / routed_scale) * a * (1.0 - a)
        for dg, a in zip((dg0, dg1), affin)
    ]
    for e in range(EXPERTS):
        share = jnp.where(choices[1][0] == e, grad_logit[0], 0.0)
        share = share + jnp.where(choices[1][1] == e, grad_logit[1], 0.0)
        grad_normed = grad_normed + share * router_rows[e : e + 1].astype(f32)
    scaled = grad_normed * gain
    mean = jnp.mean(scaled * s, -1, keepdims=True)
    grad = cot + inverse * scaled - s * inverse * inverse * inverse * mean
    return layer_out.astype(bf16), grad.astype(bf16)


def combine_first_kernel(
    in_ref, x_ref, s_ref, c_ref, stat_ref, fid_ref, bid_ref, gain_ref, router_ref, y_ref, b_ref
):
    y, b = combine(
        in_ref, x_ref[0].astype(f32), s_ref[0, 0].astype(f32), c_ref[0].astype(f32),
        stat_ref[0], stat_ref[1], fid_ref[0, 0], bid_ref[0, 0],
        gain_ref[...].astype(f32), router_ref[...],
    )
    y_ref[...] = y
    b_ref[...] = b


def combine_second_kernel(
    in_ref, x_ref, s_ref, c_ref, stat_ref, x_stat_ref, fid_ref, bid_ref, gain_ref, router_ref,
    y0_ref, b0_ref, y_ref, b_ref,
):
    y, b = combine(
        in_ref, x_ref[...].astype(f32), s_ref[1, 0].astype(f32), c_ref[...].astype(f32),
        x_stat_ref[...], stat_ref[2], fid_ref[1, 0], bid_ref[1, 0],
        gain_ref[...].astype(f32), router_ref[...],
    )
    y_ref[0, 0] = y0_ref[...]
    b_ref[0, 0] = b0_ref[...]
    y_ref[1, 0] = y
    b_ref[1, 0] = b


VMEM_BYTES = 28 * 2**20
PREPARE_BYTES = 62 * 2**20


def in_hbm(args):
    return [pltpu.with_memory_space_constraint(a, pltpu.HBM) for a in args]


def call(kernel, outs, *args, smem=0, weights=()):
    spec = pl.BlockSpec(memory_space=pltpu.VMEM)
    first = pl.BlockSpec(memory_space=pltpu.SMEM)
    far = pl.BlockSpec(memory_space=pltpu.HBM)
    outs = [jax.ShapeDtypeStruct(*o) for o in outs]
    scratch = []
    if weights:
        scratch = [pltpu.VMEM(w.shape, w.dtype) for w in weights]
        scratch.append(pltpu.SemaphoreType.DMA((CHUNKS + 1,)))
    return pl.pallas_call(
        kernel,
        out_shape=outs,
        in_specs=[first] * smem + [spec] * (len(args) - smem) + [far] * len(weights),
        out_specs=[spec] * len(outs),
        scratch_shapes=scratch,
        compiler_params=pltpu.CompilerParams(vmem_limit_bytes=VMEM_BYTES),
    )(*args, *in_hbm(weights))


def swapped(block):
    return lax.ppermute(block, "core", [(0, 1), (1, 0)])


def exchanged(block):
    block = block.reshape(ROWS, block.shape[-1])
    return lax.all_to_all(block, ("x", "y"), split_axis=0, concat_axis=0, tiled=True)


def shifted(block, distance):
    count = lax.axis_size("pipe")
    route_ = [(i - distance, i) for i in range(count) if 0 <= i - distance < count]
    return lax.ppermute(block, "pipe", route_)


def per_device(
    forward_in, forward_new, grad_in, grad_new, saved_inputs, forward_ids, backward_ids,
    norm_gain, router, gate_proj, up_proj, down_proj,
):
    width = forward_in.shape[-1]
    row = (TOK, width)
    stat = (TOK, 128)
    forward_ids = forward_ids.transpose(0, 1, 3, 2)
    backward_ids = backward_ids.transpose(0, 1, 3, 2)
    router = router[0].T
    args = (forward_in, saved_inputs, grad_in, norm_gain, router, forward_ids, backward_ids)
    sent, stats = pl.pallas_call(
        prepare_kernel,
        out_shape=[jax.ShapeDtypeStruct((ROWS, width), bf16), jax.ShapeDtypeStruct((3, *stat), f32)],
        in_specs=[pl.BlockSpec(memory_space=pltpu.HBM)] * len(args),
        out_specs=[pl.BlockSpec(memory_space=pltpu.HBM), pl.BlockSpec(memory_space=pltpu.VMEM)],
        scratch_shapes=[pltpu.VMEM(a.shape, a.dtype) for a in args]
        + [
            pltpu.VMEM((ROWS // 2, width), bf16),
            pltpu.SemaphoreType.DMA((len(args),)),
            pltpu.SemaphoreType.DMA((2 * EXPERTS,)),
        ],
        compiler_params=pltpu.CompilerParams(vmem_limit_bytes=PREPARE_BYTES),
    )(*in_hbm(args))
    gates_, ups, downs = gate_proj[0], up_proj[0], down_proj[0]
    weights = (
        jnp.concatenate([w.T for w in (gates_, swapped(gates_), ups, swapped(ups))], 0),
        jnp.concatenate([downs, swapped(downs)], 0),
    )
    hidden = weights[0].shape[0]
    packed = (PAIRS, 2, BLOCK, width // 2 + PACK)

    came = exchanged(sent)
    sent, keep = call(
        experts_first_kernel, [(packed, bf16), ((SHARED, hidden), f32)], came, weights=weights
    )
    came = exchanged(sent)
    y0, b0 = call(
        combine_first_kernel, [(row, bf16)] * 2,
        came, forward_in, saved_inputs, grad_in, stats, forward_ids, backward_ids, norm_gain, router,
    )
    section = lax.axis_index("pipe").astype(jnp.int32).reshape(1, 1)
    sent, x1, c1, x1_stat = call(
        functools.partial(again_kernel, last=lax.axis_size("pipe") - 1),
        [((ROWS, width // 2), bf16), (row, bf16), (row, bf16), (stat, f32)],
        section, shifted(y0, 1), forward_new, shifted(b0, -1), grad_new, norm_gain, router,
        forward_ids, backward_ids,
        smem=1,
    )
    came = exchanged(sent)
    (sent,) = call(experts_second_kernel, [(packed, bf16)], came, keep, weights=weights)
    came = exchanged(sent)
    full = (2, 1, *row)
    return tuple(
        call(
            combine_second_kernel, [(full, bf16)] * 2,
            came, x1, saved_inputs, c1, stats, x1_stat, forward_ids, backward_ids, norm_gain, router,
            y0, b0,
        )
    )


def solution(mesh):
    split = Mesh(np.asarray(mesh.devices).reshape(-1, 4, 4, 2), ("pipe", "x", "y", "core"))
    tokens = ("x", "y", "core")
    in_specs = (
        P("pipe", tokens, None),
        P(None, tokens, None),
        P("pipe", tokens, None),
        P(None, tokens, None),
        P(None, "pipe", tokens, None),
        P(None, "pipe", tokens, None),
        P(None, "pipe", tokens, None),
        P("pipe", None),
        P("pipe", None, None),
        P("pipe", None, tokens),
        P("pipe", None, tokens),
        P("pipe", tokens, None),
    )
    out_specs = (P(None, "pipe", tokens, None), P(None, "pipe", tokens, None))
    return jax.shard_map(
        per_device, mesh=split, in_specs=in_specs, out_specs=out_specs, check_vma=False
    )
```
